32 devices in a mesh: gx: 8 (over y, x, core), gy: 4 (over z).
Axes of the slice: x: 2, y: 2, z: 4, core: 2. Of those that a mesh axis runs over, the one named last changes fastest.
Arguments:
- previous: float32 [128, 128, 2048], P('gx', 'gy'), may hold values from -1.8 to 1.8
- source: float32 [128, 128, 2048], P('gx', 'gy'), may hold values from -5 to 5
- conductivity: float32 [128, 128, 2048], P('gx', 'gy'), may hold values from 0.24 to 8.1
Outputs:
- correction: float32 [128, 128, 2048], P('gx', 'gy')
The draws below stay inside these ranges and needn't reach their ends.
All inputs are finite; a program needn't handle non-finite values.
Results may differ from the reference program's by a relative error of at most 0.000068.
Values sent between devices are 32-bit elements; how exact they have to be, the bound alone decides.
A program may use at most 320 MiB of HBM per device.

```python
import math
import jax
import jax.numpy as jnp
from jax import lax

F = 16
CSWEEPS = 32
NX = 128
NY = 128
NZ = 2048


def draw_source(key, part):
    rough_key = jax.random.fold_in(key, 11)
    wave_key = jax.random.fold_in(key, 12)
    phase_key = jax.random.fold_in(key, 13)
    block_key = jax.random.fold_in(key, 14)
    rough_part = jnp.clip(jax.random.normal(rough_key, (NX, NY, NZ), jnp.float32), -3.0, 3.0)
    block_values = jax.random.uniform(block_key, (NX // F, NY // F, NZ // F), jnp.float32, -1.2, 1.2)
    block_part = jnp.broadcast_to(block_values[:, None, :, None, :, None], (NX // F, F, NY // F, F, NZ // F, F)).reshape(NX, NY, NZ)
    waves = jax.random.randint(wave_key, (3,), 1, 3).astype(jnp.float32)
    phase_value = jax.random.uniform(phase_key, (), jnp.float32, -math.pi, math.pi)
    plane_pos = jnp.arange(NX, dtype=jnp.float32)[:, None, None] / NX
    row_pos = jnp.arange(NY, dtype=jnp.float32)[None, :, None] / NY
    col_pos = jnp.arange(NZ, dtype=jnp.float32)[None, None, :] / NZ
    angle_value = 2.0 * math.pi * (waves[0] * plane_pos + waves[1] * row_pos + waves[2] * col_pos) + phase_value
    smooth_part = 0.6 * jnp.cos(angle_value)
    return (rough_part + block_part + smooth_part).astype(jnp.float32)


def draw_conductivity(key, part):
    cell_key = jax.random.fold_in(key, 21)
    phase_key = jax.random.fold_in(key, 22)
    cell_part = jnp.exp(jax.random.uniform(cell_key, (NX, NY, NZ), jnp.float32, math.log(0.5), math.log(4.0)))
    phase_value = jax.random.uniform(phase_key, (), jnp.float32, -math.pi, math.pi)
    plane_pos = jnp.arange(NX, dtype=jnp.float32)[:, None, None] / NX
    row_pos = jnp.arange(NY, dtype=jnp.float32)[None, :, None] / NY
    smooth_part = jnp.exp(0.7 * jnp.cos(2.0 * math.pi * (plane_pos + row_pos) + phase_value))
    return (cell_part * smooth_part).astype(jnp.float32)


def levels(rng, shape, cuts, low, top_value):
    def one(dim, blocks):
        heights = jax.random.uniform(jax.random.fold_in(jax.random.fold_in(rng, 6), dim), (blocks,), jnp.float32, low / len(cuts), top_value / len(cuts))
        return jnp.repeat(jnp.exp(heights), shape[dim] // blocks).reshape((-1,) + (1,) * (len(shape) - dim - 1))

    level = one(*cuts[0])
    for cut in cuts[1:]:
        level = level * one(*cut)
    return level


def noise(key, shape, scale, bound, shards=(), kind=jnp.bfloat16):
    array = jax.random.normal(key, shape, jnp.float32) * scale
    if len(shards) > 0:
        array = levels(key, shape, shards, -0.22, 0.18) * array
    return jnp.clip(array, min=-bound, max=bound).astype(kind)


def setup_inputs(seed: int = 0) -> dict:
    arg_keys = jax.random.split(jax.random.key(seed), 4)
    return {
        "previous": noise(arg_keys[0], (NX, NY, NZ), 0.3, 1.8, ((0, 8), (1, 4)), jnp.float32),
        "source": draw_source(jax.random.fold_in(arg_keys[3], 71), 0),
        "conductivity": draw_conductivity(jax.random.fold_in(arg_keys[3], 71), 0),
    }


reaction = 0.2
damping = 0.8
coarse_factor = 0.25


def beside_all(values):
    return [jnp.roll(values, -1, 0), jnp.roll(values, 1, 0), jnp.roll(values, -1, 1), jnp.roll(values, 1, 1), jnp.roll(values, 1, 2), jnp.roll(values, -1, 2)]


def diagonal(conduct, factor):
    summed = jnp.full_like(conduct, reaction)
    for beside in beside_all(conduct):
        summed = summed + (0.5 * factor) * (conduct + beside)
    return summed


def operate(field, conduct, factor):
    result = reaction * field
    for near_field, near_cond in zip(beside_all(field), beside_all(conduct)):
        result = result + ((0.5 * factor) * (conduct + near_cond)) * (field - near_field)
    return result


def restrict(values):
    planes, rows_count, cols_count = values.shape
    return values.reshape(planes // F, F, rows_count // F, F, cols_count // F, F).mean(axis=(1, 3, 5))


def interp_matrix(coarse_count):
    fine_index = jnp.arange(coarse_count * F, dtype=jnp.int32)
    base_index = fine_index // F + 1
    offset = ((fine_index % F).astype(jnp.float32) + 0.5) / F - 0.5
    side_index = jnp.where(offset > 0, base_index + 1, base_index - 1)
    row_index = jnp.arange(coarse_count + 2, dtype=jnp.int32)[:, None]
    weight = jnp.abs(offset)
    first_part = jnp.where(row_index == base_index[None, :], 1.0 - weight, 0.0 * weight)
    return first_part + jnp.where(row_index == side_index[None, :], weight, 0.0 * weight)


def reference(previous, source, conductivity):
    diag_fine = diagonal(conductivity, 1.0)
    residual = source - operate(previous, conductivity, 1.0)
    fine_corr = damping * residual / diag_fine
    for repeat in range(2):
        fine_corr = fine_corr + damping * (residual - operate(fine_corr, conductivity, 1.0)) / diag_fine
    coarse_resid = restrict(residual)
    coarse_cond = restrict(conductivity)
    factor = coarse_factor
    diag_coarse = diagonal(coarse_cond, factor)
    coarse_corr = damping * coarse_resid / diag_coarse
    for repeat in range(CSWEEPS - 1):
        coarse_corr = coarse_corr + damping * (coarse_resid - operate(coarse_corr, coarse_cond, factor)) / diag_coarse
    padded = jnp.pad(coarse_corr, 1, mode="wrap")
    along_cols = jnp.einsum("abc,cz->abz", padded, interp_matrix(coarse_corr.shape[2]), precision=lax.Precision.HIGHEST)
    along_rows = jnp.einsum("abz,by->ayz", along_cols, interp_matrix(coarse_corr.shape[1]), precision=lax.Precision.HIGHEST)
    interpolated = jnp.einsum("ayz,ax->xyz", along_rows, interp_matrix(coarse_corr.shape[0]), precision=lax.Precision.HIGHEST)
    return fine_corr + interpolated
```

```python
import functools

import jax
import jax.numpy as jnp
from jax import lax
from jax.experimental import pallas as pl
from jax.experimental.pallas import tpu as pltpu
from jax.sharding import PartitionSpec as P

F = 16
CSWEEPS = 32
LANES = 128
TOP = 8

reaction = 0.2
damping = 0.8
coarse_factor = 0.25

MESH = pl.DeviceIdType.MESH
HI = lax.Precision.HIGHEST


def lane_index(shape):
    return lax.broadcasted_iota(jnp.int32, shape, len(shape) - 1)


def next_col(here, after):
    first = lane_index(here.shape) == 0
    return pltpu.roll(jnp.where(first, after, here), LANES - 1, 1)


def prev_col(before, here):
    last = lane_index(here.shape) == LANES - 1
    return pltpu.roll(jnp.where(last, before, here), 1, 1)


def main_kernel(
    nx, ny, planes, rows, chunks,
    prev_hbm, src_hbm, cond_hbm, out_hbm, cols_ref,
    cond, prev, corr1, corr2, src, wgt, cx, cy, cz,
    row_send, row_recv, acc, part, gather, coarse,
    load_sem, out_sem, send_sem, recv_sem, psend_sem, precv_sem, gsend_sem, grecv_sem,
):
    gx, gy = lax.axis_index("gx"), lax.axis_index("gy")
    body_rows = pl.ds(TOP, rows)
    up_rows = pl.ds(TOP + 1, rows)
    down_rows = pl.ds(TOP - 1, rows)
    last_row = TOP + rows - 1

    loads = ((cond_hbm, cond, True), (prev_hbm, prev, True), (src_hbm, src, False))
    for k, (hbm, buf, padded) in enumerate(loads):
        for c in range(chunks):
            part_hbm = hbm.at[:, :, pl.ds(c * LANES, LANES)]
            dst = buf.at[pl.ds(1, planes), c, body_rows, :] if padded else buf.at[:, c]
            pltpu.make_async_copy(part_hbm, dst, load_sem.at[k]).start()

    def wait_load(k):
        pltpu.make_async_copy(src, src, load_sem.at[k]).wait()

    barrier = pltpu.get_barrier_semaphore()
    for j in range(1, nx):
        pl.semaphore_signal(barrier, inc=1, device_id=(lax.rem(gx + j, nx), gy), device_id_type=MESH)
    for j in range(1, ny):
        pl.semaphore_signal(barrier, inc=1, device_id=(gx, lax.rem(gy + j, ny)), device_id_type=MESH)
    pl.semaphore_wait(barrier, nx + ny - 2)

    x_next, x_prev = (lax.rem(gx + 1, nx), gy), (lax.rem(gx + nx - 1, nx), gy)
    y_next, y_prev = (gx, lax.rem(gy + 1, ny)), (gx, lax.rem(gy + ny - 1, ny))
    fields = (cond, prev, corr1, corr2)

    def remote(source, target, sem, device):
        return pltpu.make_async_remote_copy(
            src_ref=source, dst_ref=target, send_sem=send_sem.at[sem], recv_sem=recv_sem.at[sem],
            device_id=device, device_id_type=MESH,
        )

    def plane_copies(k):
        buf = fields[k]
        return (
            remote(buf.at[1, :, body_rows, :], buf.at[planes + 1, :, body_rows, :], 4 * k, x_prev),
            remote(buf.at[planes, :, body_rows, :], buf.at[0, :, body_rows, :], 4 * k + 1, x_next),
        )

    def row_copies(k):
        return (
            remote(row_send.at[k, 0], row_recv.at[k, 0], 4 * k + 2, y_prev),
            remote(row_send.at[k, 1], row_recv.at[k, 1], 4 * k + 3, y_next),
        )

    def start_all(copies):
        for copy in copies:
            copy.start()

    def wait_recv(copies):
        for copy in copies:
            copy.wait_recv()

    def pack(k, p, c, block):
        at = (p - 1) * chunks + c
        row_send[k, 0, pl.ds(at, 1), :] = block[0:1]
        row_send[k, 1, pl.ds(at, 1), :] = block[rows - 1 : rows]

    def pack_all(k):
        buf = fields[k]

        @pl.loop(1, planes + 1)
        def _(p):
            for c in range(chunks):
                at = (p - 1) * chunks + c
                row_send[k, 0, pl.ds(at, 1), :] = buf[p, c, TOP : TOP + 1, :]
                row_send[k, 1, pl.ds(at, 1), :] = buf[p, c, last_row : last_row + 1, :]

    def unpack_all(k):
        buf = fields[k]

        @pl.loop(1, planes + 1)
        def _(p):
            for c in range(chunks):
                at = (p - 1) * chunks + c
                buf[p, c, last_row + 1 : last_row + 2, :] = row_recv[k, 0, pl.ds(at, 1), :]
                buf[p, c, TOP - 1 : TOP, :] = row_recv[k, 1, pl.ds(at, 1), :]

    for k in (0, 1):
        wait_load(k)
        start_all(plane_copies(k))
        pack_all(k)
        start_all(row_copies(k))
    acc[...] = jnp.zeros_like(acc)
    wait_load(2)
    for k in (0, 1):
        wait_recv(row_copies(k))
        unpack_all(k)

    half = rows // F

    def add_part(field, c, block):
        for r in range(half):
            piece = block[r * F : r * F + 8] + block[r * F + 8 : r * F + 16]
            at = (field * half + r) * chunks + c
            acc[at] = acc[at] + piece

    def plane_of(i):
        return lax.rem(i + 1, planes) + 1

    @pl.loop(0, planes)
    def _(i):
        p = plane_of(i)

        @pl.when(i == planes - 2)
        def _():
            wait_recv(plane_copies(0))
            wait_recv(plane_copies(1))

        def cond_at(c):
            return cond[p, c % chunks, body_rows, :]

        def prev_at(c):
            return prev[p, c % chunks, body_rows, :]

        k_here = cond_at(chunks - 1)
        k_after = cond_at(0)
        cz_before = k_here + next_col(k_here, k_after)
        q_before = cz_before * prev_at(chunks - 1)
        k_here = k_after
        v_here = prev_at(0)
        for c in range(chunks):
            k_after, v_after = cond_at(c + 1), prev_at(c + 1)
            cz_here = k_here + next_col(k_here, k_after)
            q_here = cz_here * v_here
            cz_low = prev_col(cz_before, cz_here)
            cx_high = k_here + cond[p + 1, c, body_rows, :]
            cx_low = k_here + cond[p - 1, c, body_rows, :]
            cy_high = k_here + cond[p, c, up_rows, :]
            cy_low = k_here + cond[p, c, down_rows, :]
            cz[p - 1, c] = cz_here
            cx[p, c] = cx_high
            cx[p - 1, c] = cx_low
            cy[p - 1, c, body_rows, :] = cy_high
            cy[p - 1, c, TOP - 1 : TOP, :] = cy_low[0:1]
            twice_diag = (((cx_high + cx_low) + (cy_high + cy_low)) + (cz_here + cz_low)) + 2 * reaction
            total = (
                (cx_high * prev[p + 1, c, body_rows, :] + cx_low * prev[p - 1, c, body_rows, :])
                + (cy_high * prev[p, c, up_rows, :] + cy_low * prev[p, c, down_rows, :])
            ) + (cz_here * next_col(v_here, v_after) + prev_col(q_before, q_here))
            resid = src[p - 1, c] - 0.5 * (twice_diag * v_here - total)
            weight = damping / twice_diag
            first = (2.0 * weight) * resid
            wgt[p - 1, c] = weight
            corr1[p, c, body_rows, :] = first
            pack(2, p, c, first)
            add_part(0, c, resid)
            add_part(1, c, k_here)
            k_here, v_here, cz_before, q_before = k_after, v_after, cz_here, q_here

    start_all(plane_copies(2))
    start_all(row_copies(2))

    lines = 2 * half * chunks
    sums = jnp.sum(acc[...], axis=1)
    per_chunk = LANES // F
    lane_row = lax.broadcasted_iota(jnp.int32, (LANES, LANES), 0)
    lane_col = lax.broadcasted_iota(jnp.int32, (LANES, LANES), 1)
    pool = jnp.where(lax.rem(lane_col, per_chunk) == lax.div(lane_row, F), 1.0, 0.0)
    pooled = jnp.dot(sums, pool, precision=HI, preferred_element_type=jnp.float32)
    line_row = lax.broadcasted_iota(jnp.int32, (lines, LANES), 0)
    line_col = lax.broadcasted_iota(jnp.int32, (lines, LANES), 1)
    pooled = jnp.where(lax.div(line_col, per_chunk) == lax.rem(line_row, chunks), pooled, 0.0)
    small = jnp.sum(pooled.reshape(2 * half, chunks, LANES), axis=1) * (1.0 / (F * F * F))
    part[gy, 0 : 2 * half, :] = small

    def part_copy(j):
        return pltpu.make_async_remote_copy(
            src_ref=part.at[gy], dst_ref=part.at[gy], send_sem=psend_sem.at[j], recv_sem=precv_sem.at[j],
            device_id=(gx, lax.rem(gy + j, ny)), device_id_type=MESH,
        )

    def part_arrival(j):
        at = lax.rem(gy + ny - j, ny)
        return pltpu.make_async_remote_copy(
            src_ref=part.at[at], dst_ref=part.at[at], send_sem=psend_sem.at[j], recv_sem=precv_sem.at[j],
            device_id=(gx, lax.rem(gy + j, ny)), device_id_type=MESH,
        )

    def gather_copy(j):
        return pltpu.make_async_remote_copy(
            src_ref=gather.at[gx], dst_ref=gather.at[gx], send_sem=gsend_sem.at[j], recv_sem=grecv_sem.at[j],
            device_id=(lax.rem(gx + j, nx), gy), device_id_type=MESH,
        )

    def gather_arrival(j):
        at = lax.rem(gx + nx - j, nx)
        return pltpu.make_async_remote_copy(
            src_ref=gather.at[at], dst_ref=gather.at[at], send_sem=gsend_sem.at[j], recv_sem=grecv_sem.at[j],
            device_id=(lax.rem(gx + j, nx), gy), device_id_type=MESH,
        )

    for j in range(1, ny):
        part_copy(j).start()

    wait_recv(row_copies(2))
    unpack_all(2)

    for j in range(1, ny):
        part_arrival(j).wait_recv()
    for y in range(ny):
        for f in range(2):
            gather[gx, f, y * half : (y + 1) * half, :] = part[y, f * half : (f + 1) * half, :]
    for j in range(1, nx):
        gather_copy(j).start()

    def sweep(k, buf, write):
        @pl.loop(0, planes)
        def _(i):
            p = plane_of(i)

            @pl.when(i == planes - 2)
            def _():
                wait_recv(plane_copies(k))

            def at(c):
                return buf[p, c % chunks, body_rows, :]

            q_before = cz[p - 1, chunks - 1] * at(chunks - 1)
            here = at(0)
            for c in range(chunks):
                after = at(c + 1)
                cz_here = cz[p - 1, c]
                q_here = cz_here * here
                total = (
                    (cx[p, c] * buf[p + 1, c, body_rows, :] + cx[p - 1, c] * buf[p - 1, c, body_rows, :])
                    + (
                        cy[p - 1, c, body_rows, :] * buf[p, c, up_rows, :]
                        + cy[p - 1, c, down_rows, :] * buf[p, c, down_rows, :]
                    )
                ) + (cz_here * next_col(here, after) + prev_col(q_before, q_here))
                write(p, c, here, wgt[p - 1, c] * total)
                here, q_before = after, q_here

            if k == 3:
                @pl.when((lax.rem(i, 4) == 3) & (i < planes - 1))
                def _():
                    store_planes(i - 2, 4)

    def write_second(p, c, here, term):
        second = (1.0 + (1.0 - damping)) * here + term
        corr2[p, c, body_rows, :] = second
        pack(3, p, c, second)

    sweep(2, corr1, write_second)
    start_all(plane_copies(3))
    start_all(row_copies(3))

    for j in range(1, nx):
        gather_arrival(j).wait_recv()
    crows = ny * half
    resid = gather[:, 0]
    ccond = gather[:, 1]

    def around(v):
        return (
            jnp.concatenate([v[1:], v[:1]], axis=0), jnp.concatenate([v[-1:], v[:-1]], axis=0),
            pltpu.roll(v, crows - 1, 1), pltpu.roll(v, 1, 1),
            pltpu.roll(v, 1, 2), pltpu.roll(v, LANES - 1, 2),
        )

    ccoup = [(0.5 * coarse_factor) * (ccond + near) for near in around(ccond)]
    cdiag = jnp.full_like(ccond, reaction)
    for one in ccoup:
        cdiag = cdiag + one
    cwgt = damping / cdiag
    ccoup = [cwgt * one for one in ccoup]
    cfirst = cwgt * resid

    def coarse_step(_, v):
        result = (1.0 - damping) * v + cfirst
        for one, near in zip(ccoup, around(v)):
            result = result + one * near
        return result

    coarse[...] = lax.fori_loop(0, CSWEEPS - 1, coarse_step, cfirst)
    turn = lax.rem(2 * crows + 1 - gy * half, crows)
    block = []
    for a in range(3):
        plane = coarse[lax.rem(gx + nx - 1 + a, nx)]
        block.append(pltpu.roll(plane, turn, 0)[0:8])
    block = jnp.concatenate(block, axis=0)
    ccols = chunks * LANES // F
    for c in range(chunks):
        fine = c * LANES + lane_col
        base = lax.div(fine, F)
        offset = (lax.rem(fine, F).astype(jnp.float32) + 0.5) / F - 0.5
        side = lax.rem(jnp.where(offset > 0, base + 1, base + ccols - 1), ccols)
        spread = jnp.where(lane_row == base, 1.0 - jnp.abs(offset), 0.0)
        spread = spread + jnp.where(lane_row == side, jnp.abs(offset), 0.0)
        cols_ref[:, c * LANES : (c + 1) * LANES] = jnp.dot(
            block, spread, precision=HI, preferred_element_type=jnp.float32
        )

    wait_recv(row_copies(3))
    unpack_all(3)

    def out_copy(c, start, count):
        return pltpu.make_async_copy(
            src.at[pl.ds(start, count), c],
            out_hbm.at[pl.ds(start, count), :, pl.ds(c * LANES, LANES)],
            out_sem,
        )

    def store_planes(start, count):
        for c in range(chunks):
            out_copy(c, start, count).start()

    def write_third(p, c, here, term):
        src[p - 1, c] = ((1.0 - damping) * here + corr1[p, c, body_rows, :]) + term

    sweep(3, corr2, write_third)
    store_planes(planes - 3, 3)
    store_planes(0, 1)

    for k in range(4):
        for copy in plane_copies(k) + row_copies(k):
            copy.wait_send()
    for j in range(1, ny):
        part_copy(j).wait_send()
    for j in range(1, nx):
        gather_copy(j).wait_send()
    pltpu.make_async_copy(src, src, out_sem).wait()


def add_kernel(step_planes, rows, fine_ref, cols_ref, out_ref, across):
    step = pl.program_id(0)
    half = rows // F

    @pl.when(step == 0)
    def _():
        row = lax.broadcasted_iota(jnp.int32, (rows, LANES), 0)
        base = lax.div(row, F) + 1
        offset = (lax.rem(row, F).astype(jnp.float32) + 0.5) / F - 0.5
        side = jnp.where(offset > 0, base + 1, base - 1)
        weights = [
            jnp.where(base == b, 1.0 - jnp.abs(offset), 0.0) + jnp.where(side == b, jnp.abs(offset), 0.0)
            for b in range(half + 2)
        ]
        for a in range(3):
            for c in range(cols_ref.shape[1] // LANES):
                at = pl.ds(c * LANES, LANES)
                total = weights[0] * cols_ref[8 * a : 8 * a + 1, at]
                for b in range(1, half + 2):
                    total = total + weights[b] * cols_ref[8 * a + b : 8 * a + b + 1, at]
                across[a, :, at] = total

    for q in range(step_planes):
        plane = step * step_planes + q
        offset = (plane.astype(jnp.float32) + 0.5) / F - 0.5
        side = jnp.where(offset > 0, 2, 0)
        weight = jnp.abs(offset)
        out_ref[q] = fine_ref[q] + ((1.0 - weight) * across[1] + weight * across[side])


def per_device(nx, ny, previous, source, conductivity):
    planes, rows, cols = previous.shape
    chunks = cols // LANES
    half = rows // F
    f32 = jnp.float32
    padded = pltpu.VMEM((planes + 2, chunks, rows + 16, LANES), f32)
    plain = pltpu.VMEM((planes, chunks, rows, LANES), f32)
    any_spec = pl.BlockSpec(memory_space=pl.ANY)
    fine, along = pl.pallas_call(
        functools.partial(main_kernel, nx, ny, planes, rows, chunks),
        out_shape=(
            jax.ShapeDtypeStruct((planes, rows, cols), f32),
            jax.ShapeDtypeStruct((24, cols), f32),
        ),
        in_specs=[any_spec] * 3,
        out_specs=(any_spec, pl.BlockSpec(memory_space=pltpu.VMEM)),
        scratch_shapes=[
            padded, padded, padded, padded, plain, plain,
            pltpu.VMEM((planes + 1, chunks, rows, LANES), f32),
            pltpu.VMEM((planes, chunks, rows + 8, LANES), f32),
            plain,
            pltpu.VMEM((4, 2, planes * chunks, LANES), f32),
            pltpu.VMEM((4, 2, planes * chunks, LANES), f32),
            pltpu.VMEM((2 * half * chunks, 8, LANES), f32),
            pltpu.VMEM((ny, 8, LANES), f32),
            pltpu.VMEM((nx, 2, ny * half, LANES), f32),
            pltpu.VMEM((nx, ny * half, LANES), f32),
            pltpu.SemaphoreType.DMA((3,)),
            pltpu.SemaphoreType.DMA,
            pltpu.SemaphoreType.DMA((16,)),
            pltpu.SemaphoreType.DMA((16,)),
            pltpu.SemaphoreType.DMA((ny,)),
            pltpu.SemaphoreType.DMA((ny,)),
            pltpu.SemaphoreType.DMA((nx,)),
            pltpu.SemaphoreType.DMA((nx,)),
        ],
        compiler_params=pltpu.CompilerParams(
            collective_id=0, has_side_effects=True, vmem_limit_bytes=60 * 1024 * 1024
        ),
        name="correction_main",
    )(previous, source, conductivity)
    step_planes = 4
    return pl.pallas_call(
        functools.partial(add_kernel, step_planes, rows),
        out_shape=jax.ShapeDtypeStruct((planes, rows, cols), f32),
        grid=(planes // step_planes,),
        in_specs=[
            pl.BlockSpec((step_planes, rows, cols), lambda i: (i, 0, 0)),
            pl.BlockSpec((24, cols), lambda i: (0, 0)),
        ],
        out_specs=pl.BlockSpec((step_planes, rows, cols), lambda i: (i, 0, 0)),
        scratch_shapes=[pltpu.VMEM((3, rows, cols), f32)],
        compiler_params=pltpu.CompilerParams(vmem_limit_bytes=32 * 1024 * 1024),
        name="interpolate_add",
    )(fine, along)


def solution(mesh):
    placed = P("gx", "gy", None)
    nx, ny = mesh.shape["gx"], mesh.shape["gy"]
    return jax.shard_map(
        functools.partial(per_device, nx, ny), mesh=mesh, in_specs=(placed,) * 3, out_specs=placed,
        check_vma=False,
    )
```

```python
import functools

import jax
import jax.numpy as jnp
from jax import lax
from jax.experimental import pallas as pl
from jax.experimental.pallas import tpu as pltpu
from jax.sharding import PartitionSpec as P

F = 16
CSWEEPS = 32
LANES = 128
TOP = 8

reaction = 0.2
damping = 0.8
coarse_factor = 0.25

MESH = pl.DeviceIdType.MESH
HI = lax.Precision.HIGHEST


def lane_index(shape):
    return lax.broadcasted_iota(jnp.int32, shape, len(shape) - 1)


def next_col(here, after):
    first = lane_index(here.shape) == 0
    return pltpu.roll(jnp.where(first, after, here), LANES - 1, 1)


def prev_col(before, here):
    last = lane_index(here.shape) == LANES - 1
    return pltpu.roll(jnp.where(last, before, here), 1, 1)


def main_kernel(
    nx, ny, planes, rows, chunks,
    prev_hbm, src_hbm, cond_hbm, out_hbm, cols_ref,
    cond, prev, corr1, corr2, src, wgt, cx, cy, cz,
    row_send, row_recv, acc, part, gather, coarse,
    load_sem, out_sem, send_sem, recv_sem, psend_sem, precv_sem, gsend_sem, grecv_sem,
):
    gx, gy = lax.axis_index("gx"), lax.axis_index("gy")
    body_rows = pl.ds(TOP, rows)
    last_row = TOP + rows - 1
    inner = planes - 2
    steps = 2 * planes

    def place_of(i):
        late = lax.div(i, 2 * inner)
        past = i - 2 * inner
        edge = (1 - late) * lax.div(i, inner) + late * lax.rem(past, 2)
        order = (1 - late) * lax.rem(i, inner) + late * (inner + lax.div(past, 2))
        return lax.rem(order + 1, planes) + 1, order, edge

    def tiles(edge):
        low = TOP + rows // 2 - 8 - (rows // 2 - 8) * edge
        high = TOP + rows // 2 + (rows // 2 - 8) * edge
        return pl.multiple_of(low, 8), pl.multiple_of(high, 8)

    def get(ref, p, c, at, shift=0):
        return jnp.concatenate([ref[p, c, pl.ds(t + shift, 8), :] for t in at], axis=0)

    def put(ref, p, c, at, block):
        ref[p, c, pl.ds(at[0], 8), :] = block[0:8]
        ref[p, c, pl.ds(at[1], 8), :] = block[8:16]

    loads = ((cond_hbm, cond, True), (prev_hbm, prev, True), (src_hbm, src, False))
    for k, (hbm, buf, padded) in enumerate(loads):
        for c in range(chunks):
            part_hbm = hbm.at[:, :, pl.ds(c * LANES, LANES)]
            dst = buf.at[pl.ds(1, planes), c, body_rows, :] if padded else buf.at[:, c]
            pltpu.make_async_copy(part_hbm, dst, load_sem.at[k]).start()

    def wait_load(k):
        pltpu.make_async_copy(src, src, load_sem.at[k]).wait()

    barrier = pltpu.get_barrier_semaphore()
    for j in range(1, nx):
        pl.semaphore_signal(barrier, inc=1, device_id=(lax.rem(gx + j, nx), gy), device_id_type=MESH)
    for j in range(1, ny):
        pl.semaphore_signal(barrier, inc=1, device_id=(gx, lax.rem(gy + j, ny)), device_id_type=MESH)
    pl.semaphore_wait(barrier, nx + ny - 2)

    x_next, x_prev = (lax.rem(gx + 1, nx), gy), (lax.rem(gx + nx - 1, nx), gy)
    y_next, y_prev = (gx, lax.rem(gy + 1, ny)), (gx, lax.rem(gy + ny - 1, ny))
    fields = (cond, prev, corr1, corr2)

    def remote(source, target, sem, device):
        return pltpu.make_async_remote_copy(
            src_ref=source, dst_ref=target, send_sem=send_sem.at[sem], recv_sem=recv_sem.at[sem],
            device_id=device, device_id_type=MESH,
        )

    def plane_copies(k):
        buf = fields[k]
        return (
            remote(buf.at[1, :, body_rows, :], buf.at[planes + 1, :, body_rows, :], 2 * k, x_prev),
            remote(buf.at[planes, :, body_rows, :], buf.at[0, :, body_rows, :], 2 * k + 1, x_next),
        )

    cut = inner * chunks

    def row_copies(k, late):
        lines = pl.ds(cut, 2 * chunks) if late else pl.ds(0, cut)
        sem = 16 + 4 * k + 2 * late
        return (
            remote(row_send.at[k, 0, lines], row_recv.at[k, 0, lines], sem, y_prev),
            remote(row_send.at[k, 1, lines], row_recv.at[k, 1, lines], sem + 1, y_next),
        )

    def start_all(copies):
        for copy in copies:
            copy.start()

    def wait_recv(copies):
        for copy in copies:
            copy.wait_recv()

    def pack(k, order, c, block):
        at = order * chunks + c
        row_send[k, 0, pl.ds(at, 1), :] = block[0:1]
        row_send[k, 1, pl.ds(at, 1), :] = block[15:16]

    def pack_all(k):
        buf = fields[k]

        @pl.loop(0, planes)
        def _(order):
            p = lax.rem(order + 1, planes) + 1
            for c in range(chunks):
                at = order * chunks + c
                row_send[k, 0, pl.ds(at, 1), :] = buf[p, c, TOP : TOP + 1, :]
                row_send[k, 1, pl.ds(at, 1), :] = buf[p, c, last_row : last_row + 1, :]

    def unpack(k, first, last):
        buf = fields[k]

        @pl.loop(first, last)
        def _(order):
            p = lax.rem(order + 1, planes) + 1
            for c in range(chunks):
                at = order * chunks + c
                buf[p, c, last_row + 1 : last_row + 2, :] = row_recv[k, 0, pl.ds(at, 1), :]
                buf[p, c, TOP - 1 : TOP, :] = row_recv[k, 1, pl.ds(at, 1), :]

    def arrivals(i, ks, sent=None):
        @pl.when(i == inner)
        def _():
            for k in ks:
                wait_recv(row_copies(k, 0))
                unpack(k, 0, inner)

        @pl.when(i == 2 * inner)
        def _():
            if sent is not None:
                start_all(row_copies(sent, 0))
            for k in ks:
                wait_recv(row_copies(k, 1))
                unpack(k, inner, planes)
                wait_recv(plane_copies(k))

    for k in (0, 1):
        wait_load(k)
        start_all(plane_copies(k))
        pack_all(k)
        start_all(row_copies(k, 0))
        start_all(row_copies(k, 1))
    acc[...] = jnp.zeros_like(acc)
    wait_load(2)

    half = rows // F

    def add_part(field, c, block):
        for r in range(half):
            at = (field * half + r) * chunks + c
            acc[at] = acc[at] + block[8 * r : 8 * r + 8]

    @pl.loop(0, steps)
    def _(i):
        p, order, edge = place_of(i)
        at = tiles(edge)
        flat = tuple(pl.multiple_of(t - TOP, 8) for t in at)
        arrivals(i, (0, 1), 2)

        def cond_at(c):
            return get(cond, p, c % chunks, at)

        def prev_at(c):
            return get(prev, p, c % chunks, at)

        k_here = cond_at(chunks - 1)
        k_after = cond_at(0)
        cz_before = k_here + next_col(k_here, k_after)
        q_before = cz_before * prev_at(chunks - 1)
        k_here = k_after
        v_here = prev_at(0)
        for c in range(chunks):
            k_after, v_after = cond_at(c + 1), prev_at(c + 1)
            cz_here = k_here + next_col(k_here, k_after)
            q_here = cz_here * v_here
            cz_low = prev_col(cz_before, cz_here)
            cx_high = k_here + get(cond, p + 1, c, at)
            cx_low = k_here + get(cond, p - 1, c, at)
            cy_high = k_here + get(cond, p, c, at, 1)
            cy_low = k_here + get(cond, p, c, at, -1)
            put(cz, p - 1, c, flat, cz_here)
            put(cx, p, c, flat, cx_high)
            put(cx, p - 1, c, flat, cx_low)
            put(cy, p - 1, c, at, cy_high)
            cy[p - 1, c, pl.ds(at[0] - 1, 1), :] = cy_low[0:1]
            twice_diag = (((cx_high + cx_low) + (cy_high + cy_low)) + (cz_here + cz_low)) + 2 * reaction
            total = (
                (cx_high * get(prev, p + 1, c, at) + cx_low * get(prev, p - 1, c, at))
                + (cy_high * get(prev, p, c, at, 1) + cy_low * get(prev, p, c, at, -1))
            ) + (cz_here * next_col(v_here, v_after) + prev_col(q_before, q_here))
            resid = get(src, p - 1, c, flat) - 0.5 * (twice_diag * v_here - total)
            weight = damping / twice_diag
            first = (2.0 * weight) * resid
            put(wgt, p - 1, c, flat, weight)
            put(corr1, p, c, at, first)
            pack(2, order, c, first)
            add_part(0, c, resid)
            add_part(1, c, k_here)
            k_here, v_here, cz_before, q_before = k_after, v_after, cz_here, q_here

    start_all(plane_copies(2))
    start_all(row_copies(2, 1))

    lines = 2 * half * chunks
    sums = jnp.sum(acc[...], axis=1)
    per_chunk = LANES // F
    lane_row = lax.broadcasted_iota(jnp.int32, (LANES, LANES), 0)
    lane_col = lax.broadcasted_iota(jnp.int32, (LANES, LANES), 1)
    pool = jnp.where(lax.rem(lane_col, per_chunk) == lax.div(lane_row, F), 1.0, 0.0)
    pooled = jnp.dot(sums, pool, precision=HI, preferred_element_type=jnp.float32)
    line_row = lax.broadcasted_iota(jnp.int32, (lines, LANES), 0)
    line_col = lax.broadcasted_iota(jnp.int32, (lines, LANES), 1)
    pooled = jnp.where(lax.div(line_col, per_chunk) == lax.rem(line_row, chunks), pooled, 0.0)
    small = jnp.sum(pooled.reshape(2 * half, chunks, LANES), axis=1) * (1.0 / (F * F * F))
    part[gy, 0 : 2 * half, :] = small

    def part_copy(j):
        return pltpu.make_async_remote_copy(
            src_ref=part.at[gy], dst_ref=part.at[gy], send_sem=psend_sem.at[j], recv_sem=precv_sem.at[j],
            device_id=(gx, lax.rem(gy + j, ny)), device_id_type=MESH,
        )

    def part_arrival(j):
        at = lax.rem(gy + ny - j, ny)
        return pltpu.make_async_remote_copy(
            src_ref=part.at[at], dst_ref=part.at[at], send_sem=psend_sem.at[j], recv_sem=precv_sem.at[j],
            device_id=(gx, lax.rem(gy + j, ny)), device_id_type=MESH,
        )

    def gather_copy(j):
        return pltpu.make_async_remote_copy(
            src_ref=gather.at[gx], dst_ref=gather.at[gx], send_sem=gsend_sem.at[j], recv_sem=grecv_sem.at[j],
            device_id=(lax.rem(gx + j, nx), gy), device_id_type=MESH,
        )

    def gather_arrival(j):
        at = lax.rem(gx + nx - j, nx)
        return pltpu.make_async_remote_copy(
            src_ref=gather.at[at], dst_ref=gather.at[at], send_sem=gsend_sem.at[j], recv_sem=grecv_sem.at[j],
            device_id=(lax.rem(gx + j, nx), gy), device_id_type=MESH,
        )

    for j in range(1, ny):
        part_copy(j).start()

    def pass_on():
        for j in range(1, ny):
            part_arrival(j).wait_recv()
        for y in range(ny):
            for f in range(2):
                gather[gx, f, y * half : (y + 1) * half, :] = part[y, f * half : (f + 1) * half, :]
        for j in range(1, nx):
            gather_copy(j).start()

    def sweep(k, buf, write, sent=None):
        @pl.loop(0, steps)
        def _(i):
            p, order, edge = place_of(i)
            at = tiles(edge)
            flat = tuple(pl.multiple_of(t - TOP, 8) for t in at)
            if k == 2:
                pl.when(i == inner // 2)(pass_on)
            arrivals(i, (k,), sent)

            def here_at(c):
                return get(buf, p, c % chunks, at)

            q_before = get(cz, p - 1, chunks - 1, flat) * here_at(chunks - 1)
            here = here_at(0)
            for c in range(chunks):
                after = here_at(c + 1)
                cz_here = get(cz, p - 1, c, flat)
                q_here = cz_here * here
                total = (
                    (get(cx, p, c, flat) * get(buf, p + 1, c, at) + get(cx, p - 1, c, flat) * get(buf, p - 1, c, at))
                    + (
                        get(cy, p - 1, c, at) * get(buf, p, c, at, 1)
                        + get(cy, p - 1, c, at, -1) * get(buf, p, c, at, -1)
                    )
                ) + (cz_here * next_col(here, after) + prev_col(q_before, q_here))
                write(p, order, c, at, flat, here, get(wgt, p - 1, c, flat) * total)
                here, q_before = after, q_here

            if k == 3:
                @pl.when((i >= inner) & (i < 2 * inner) & (lax.rem(i - inner, 4) == 3))
                def _():
                    store_planes(i - inner - 2, 4)

    def write_second(p, order, c, at, flat, here, term):
        second = (1.0 + (1.0 - damping)) * here + term
        put(corr2, p, c, at, second)
        pack(3, order, c, second)

    sweep(2, corr1, write_second, 3)
    start_all(plane_copies(3))
    start_all(row_copies(3, 1))

    for j in range(1, nx):
        gather_arrival(j).wait_recv()
    crows = ny * half
    resid = gather[:, 0]
    ccond = gather[:, 1]

    def around(v):
        return (
            jnp.concatenate([v[1:], v[:1]], axis=0), jnp.concatenate([v[-1:], v[:-1]], axis=0),
            pltpu.roll(v, crows - 1, 1), pltpu.roll(v, 1, 1),
            pltpu.roll(v, 1, 2), pltpu.roll(v, LANES - 1, 2),
        )

    ccoup = [(0.5 * coarse_factor) * (ccond + near) for near in around(ccond)]
    cdiag = jnp.full_like(ccond, reaction)
    for one in ccoup:
        cdiag = cdiag + one
    cwgt = damping / cdiag
    ccoup = [cwgt * one for one in ccoup]
    cfirst = cwgt * resid

    def coarse_step(_, v):
        result = (1.0 - damping) * v + cfirst
        for one, near in zip(ccoup, around(v)):
            result = result + one * near
        return result

    coarse[...] = lax.fori_loop(0, CSWEEPS - 1, coarse_step, cfirst)
    turn = lax.rem(2 * crows + 1 - gy * half, crows)
    block = []
    for a in range(3):
        plane = coarse[lax.rem(gx + nx - 1 + a, nx)]
        block.append(pltpu.roll(plane, turn, 0)[0:8])
    block = jnp.concatenate(block, axis=0)
    ccols = chunks * LANES // F
    for c in range(chunks):
        fine = c * LANES + lane_col
        base = lax.div(fine, F)
        offset = (lax.rem(fine, F).astype(jnp.float32) + 0.5) / F - 0.5
        side = lax.rem(jnp.where(offset > 0, base + 1, base + ccols - 1), ccols)
        spread = jnp.where(lane_row == base, 1.0 - jnp.abs(offset), 0.0)
        spread = spread + jnp.where(lane_row == side, jnp.abs(offset), 0.0)
        cols_ref[:, c * LANES : (c + 1) * LANES] = jnp.dot(
            block, spread, precision=HI, preferred_element_type=jnp.float32
        )

    def out_copy(c, start, count):
        return pltpu.make_async_copy(
            src.at[pl.ds(start, count), c],
            out_hbm.at[pl.ds(start, count), :, pl.ds(c * LANES, LANES)],
            out_sem,
        )

    def store_planes(start, count):
        for c in range(chunks):
            out_copy(c, start, count).start()

    def write_third(p, order, c, at, flat, here, term):
        put(src, p - 1, c, flat, ((1.0 - damping) * here + get(corr1, p, c, at)) + term)

    sweep(3, corr2, write_third)
    store_planes(planes - 3, 3)
    store_planes(0, 1)

    for k in range(4):
        for copy in plane_copies(k) + row_copies(k, 0) + row_copies(k, 1):
            copy.wait_send()
    for j in range(1, ny):
        part_copy(j).wait_send()
    for j in range(1, nx):
        gather_copy(j).wait_send()
    pltpu.make_async_copy(src, src, out_sem).wait()


def add_kernel(step_planes, rows, fine_ref, cols_ref, out_ref, across):
    step = pl.program_id(0)
    half = rows // F

    @pl.when(step == 0)
    def _():
        row = lax.broadcasted_iota(jnp.int32, (rows, LANES), 0)
        base = lax.div(row, F) + 1
        offset = (lax.rem(row, F).astype(jnp.float32) + 0.5) / F - 0.5
        side = jnp.where(offset > 0, base + 1, base - 1)
        weights = [
            jnp.where(base == b, 1.0 - jnp.abs(offset), 0.0) + jnp.where(side == b, jnp.abs(offset), 0.0)
            for b in range(half + 2)
        ]
        for a in range(3):
            for c in range(cols_ref.shape[1] // LANES):
                at = pl.ds(c * LANES, LANES)
                total = weights[0] * cols_ref[8 * a : 8 * a + 1, at]
                for b in range(1, half + 2):
                    total = total + weights[b] * cols_ref[8 * a + b : 8 * a + b + 1, at]
                across[a, :, at] = total

    for q in range(step_planes):
        plane = step * step_planes + q
        offset = (plane.astype(jnp.float32) + 0.5) / F - 0.5
        side = jnp.where(offset > 0, 2, 0)
        weight = jnp.abs(offset)
        out_ref[q] = fine_ref[q] + ((1.0 - weight) * across[1] + weight * across[side])


def per_device(nx, ny, previous, source, conductivity):
    planes, rows, cols = previous.shape
    chunks = cols // LANES
    half = rows // F
    f32 = jnp.float32
    padded = pltpu.VMEM((planes + 2, chunks, rows + 16, LANES), f32)
    plain = pltpu.VMEM((planes, chunks, rows, LANES), f32)
    any_spec = pl.BlockSpec(memory_space=pl.ANY)
    fine, along = pl.pallas_call(
        functools.partial(main_kernel, nx, ny, planes, rows, chunks),
        out_shape=(
            jax.ShapeDtypeStruct((planes, rows, cols), f32),
            jax.ShapeDtypeStruct((24, cols), f32),
        ),
        in_specs=[any_spec] * 3,
        out_specs=(any_spec, pl.BlockSpec(memory_space=pltpu.VMEM)),
        scratch_shapes=[
            padded, padded, padded, padded, plain, plain,
            pltpu.VMEM((planes + 1, chunks, rows, LANES), f32),
            pltpu.VMEM((planes, chunks, rows + 8, LANES), f32),
            plain,
            pltpu.VMEM((4, 2, planes * chunks, LANES), f32),
            pltpu.VMEM((4, 2, planes * chunks, LANES), f32),
            pltpu.VMEM((2 * half * chunks, 8, LANES), f32),
            pltpu.VMEM((ny, 8, LANES), f32),
            pltpu.VMEM((nx, 2, ny * half, LANES), f32),
            pltpu.VMEM((nx, ny * half, LANES), f32),
            pltpu.SemaphoreType.DMA((3,)),
            pltpu.SemaphoreType.DMA,
            pltpu.SemaphoreType.DMA((32,)),
            pltpu.SemaphoreType.DMA((32,)),
            pltpu.SemaphoreType.DMA((ny,)),
            pltpu.SemaphoreType.DMA((ny,)),
            pltpu.SemaphoreType.DMA((nx,)),
            pltpu.SemaphoreType.DMA((nx,)),
        ],
        compiler_params=pltpu.CompilerParams(
            collective_id=0, has_side_effects=True, vmem_limit_bytes=60 * 1024 * 1024
        ),
        name="correction_main",
    )(previous, source, conductivity)
    step_planes = 4
    return pl.pallas_call(
        functools.partial(add_kernel, step_planes, rows),
        out_shape=jax.ShapeDtypeStruct((planes, rows, cols), f32),
        grid=(planes // step_planes,),
        in_specs=[
            pl.BlockSpec((step_planes, rows, cols), lambda i: (i, 0, 0)),
            pl.BlockSpec((24, cols), lambda i: (0, 0)),
        ],
        out_specs=pl.BlockSpec((step_planes, rows, cols), lambda i: (i, 0, 0)),
        scratch_shapes=[pltpu.VMEM((3, rows, cols), f32)],
        compiler_params=pltpu.CompilerParams(vmem_limit_bytes=60 * 1024 * 1024),
        name="interpolate_add",
    )(fine, along)


def solution(mesh):
    placed = P("gx", "gy", None)
    nx, ny = mesh.shape["gx"], mesh.shape["gy"]
    return jax.shard_map(
        functools.partial(per_device, nx, ny), mesh=mesh, in_specs=(placed,) * 3, out_specs=placed,
        check_vma=False,
    )
```

```python
import functools

import jax
import jax.numpy as jnp
from jax import lax
from jax.experimental import pallas as pl
from jax.experimental.pallas import tpu as pltpu
from jax.sharding import PartitionSpec as P

F = 16
CSWEEPS = 32
LANES = 128
TOP = 8

reaction = 0.2
damping = 0.8
coarse_factor = 0.25

MESH = pl.DeviceIdType.MESH
HI = lax.Precision.HIGHEST


def lane_index(shape):
    return lax.broadcasted_iota(jnp.int32, shape, len(shape) - 1)


def next_col(here, after):
    first = lane_index(here.shape) == 0
    return pltpu.roll(jnp.where(first, after, here), LANES - 1, 1)


def prev_col(before, here):
    last = lane_index(here.shape) == LANES - 1
    return pltpu.roll(jnp.where(last, before, here), 1, 1)


def main_kernel(
    nx, ny, planes, rows, chunks,
    prev_hbm, src_hbm, cond_hbm, out_hbm, cols_ref,
    cond, prev, corr1, corr2, src, wgt, cx, cy, cz,
    row_send, row_recv, acc, part, gather, coarse,
    load_sem, out_sem, send_sem, recv_sem, psend_sem, precv_sem, gsend_sem, grecv_sem,
):
    gx, gy = lax.axis_index("gx"), lax.axis_index("gy")
    body_rows = pl.ds(TOP, rows)
    last_row = TOP + rows - 1
    inner = planes - 2
    steps = 2 * planes

    def place_of(i):
        late = lax.div(i, 2 * inner)
        past = i - 2 * inner
        edge = (1 - late) * lax.div(i, inner) + late * lax.rem(past, 2)
        order = (1 - late) * lax.rem(i, inner) + late * (inner + lax.div(past, 2))
        return lax.rem(order + 1, planes) + 1, order, edge

    def tiles(edge):
        low = TOP + rows // 2 - 8 - (rows // 2 - 8) * edge
        high = TOP + rows // 2 + (rows // 2 - 8) * edge
        return pl.multiple_of(low, 8), pl.multiple_of(high, 8)

    def get(ref, p, c, at, shift=0):
        return jnp.concatenate([ref[p, c, pl.ds(t + shift, 8), :] for t in at], axis=0)

    def put(ref, p, c, at, block):
        ref[p, c, pl.ds(at[0], 8), :] = block[0:8]
        ref[p, c, pl.ds(at[1], 8), :] = block[8:16]

    loads = ((cond_hbm, cond, True), (prev_hbm, prev, True), (src_hbm, src, False))
    for k, (hbm, buf, padded) in enumerate(loads):
        for c in range(chunks):
            part_hbm = hbm.at[:, :, pl.ds(c * LANES, LANES)]
            dst = buf.at[pl.ds(1, planes), c, body_rows, :] if padded else buf.at[:, c]
            pltpu.make_async_copy(part_hbm, dst, load_sem.at[k]).start()

    def wait_load(k):
        pltpu.make_async_copy(src, src, load_sem.at[k]).wait()

    barrier = pltpu.get_barrier_semaphore()
    for j in range(1, nx):
        pl.semaphore_signal(barrier, inc=1, device_id=(lax.rem(gx + j, nx), gy), device_id_type=MESH)
    for j in range(1, ny):
        pl.semaphore_signal(barrier, inc=1, device_id=(gx, lax.rem(gy + j, ny)), device_id_type=MESH)
    pl.semaphore_wait(barrier, nx + ny - 2)

    x_next, x_prev = (lax.rem(gx + 1, nx), gy), (lax.rem(gx + nx - 1, nx), gy)
    y_next, y_prev = (gx, lax.rem(gy + 1, ny)), (gx, lax.rem(gy + ny - 1, ny))
    fields = (cond, prev, corr1, corr2)

    def remote(source, target, sem, device):
        return pltpu.make_async_remote_copy(
            src_ref=source, dst_ref=target, send_sem=send_sem.at[sem], recv_sem=recv_sem.at[sem],
            device_id=device, device_id_type=MESH,
        )

    def plane_copies(k):
        buf = fields[k]
        return (
            remote(buf.at[1, :, body_rows, :], buf.at[planes + 1, :, body_rows, :], 2 * k, x_prev),
            remote(buf.at[planes, :, body_rows, :], buf.at[0, :, body_rows, :], 2 * k + 1, x_next),
        )

    cut = inner * chunks

    def row_copies(k, late):
        lines = pl.ds(cut, 2 * chunks) if late else pl.ds(0, cut)
        sem = 16 + 4 * k + 2 * late
        return (
            remote(row_send.at[k, 0, lines], row_recv.at[k, 0, lines], sem, y_prev),
            remote(row_send.at[k, 1, lines], row_recv.at[k, 1, lines], sem + 1, y_next),
        )

    def start_all(copies):
        for copy in copies:
            copy.start()

    def wait_recv(copies):
        for copy in copies:
            copy.wait_recv()

    def pack(k, order, c, block):
        at = order * chunks + c
        row_send[k, 0, pl.ds(at, 1), :] = block[0:1]
        row_send[k, 1, pl.ds(at, 1), :] = block[15:16]

    def pack_all(k):
        buf = fields[k]

        @pl.loop(0, planes)
        def _(order):
            p = lax.rem(order + 1, planes) + 1
            for c in range(chunks):
                at = order * chunks + c
                row_send[k, 0, pl.ds(at, 1), :] = buf[p, c, TOP : TOP + 1, :]
                row_send[k, 1, pl.ds(at, 1), :] = buf[p, c, last_row : last_row + 1, :]

    def unpack(k, first, last):
        buf = fields[k]

        @pl.loop(first, last)
        def _(order):
            p = lax.rem(order + 1, planes) + 1
            for c in range(chunks):
                at = order * chunks + c
                buf[p, c, last_row + 1 : last_row + 2, :] = row_recv[k, 0, pl.ds(at, 1), :]
                buf[p, c, TOP - 1 : TOP, :] = row_recv[k, 1, pl.ds(at, 1), :]

    def arrivals(i, ks, sent=None):
        @pl.when(i == inner)
        def _():
            for k in ks:
                wait_recv(row_copies(k, 0))
                unpack(k, 0, inner)

        @pl.when(i == 2 * inner)
        def _():
            if sent is not None:
                start_all(row_copies(sent, 0))
            for k in ks:
                wait_recv(row_copies(k, 1))
                unpack(k, inner, planes)
                wait_recv(plane_copies(k))

    for k in (0, 1):
        wait_load(k)
        start_all(plane_copies(k))
        pack_all(k)
        start_all(row_copies(k, 0))
        start_all(row_copies(k, 1))
    acc[...] = jnp.zeros_like(acc)

    half = rows // F

    def add_part(field, c, block):
        for r in range(half):
            at = (field * half + r) * chunks + c
            acc[at] = acc[at] + block[8 * r : 8 * r + 8]

    @pl.loop(0, steps)
    def _(i):
        p, order, edge = place_of(i)
        at = tiles(edge)
        flat = tuple(pl.multiple_of(t - TOP, 8) for t in at)
        arrivals(i, (0,))

        def cond_at(c):
            return get(cond, p, c % chunks, at)

        k_here = cond_at(chunks - 1)
        k_after = cond_at(0)
        cz_before = k_here + next_col(k_here, k_after)
        k_here = k_after
        for c in range(chunks):
            k_after = cond_at(c + 1)
            cz_here = k_here + next_col(k_here, k_after)
            cz_low = prev_col(cz_before, cz_here)
            cx_high = k_here + get(cond, p + 1, c, at)
            cx_low = k_here + get(cond, p - 1, c, at)
            cy_high = k_here + get(cond, p, c, at, 1)
            cy_low = k_here + get(cond, p, c, at, -1)
            put(cz, p - 1, c, flat, cz_here)
            put(cx, p, c, flat, cx_high)
            put(cx, p - 1, c, flat, cx_low)
            put(cy, p - 1, c, at, cy_high)
            cy[p - 1, c, pl.ds(at[0] - 1, 1), :] = cy_low[0:1]
            twice_diag = (((cx_high + cx_low) + (cy_high + cy_low)) + (cz_here + cz_low)) + 2 * reaction
            put(wgt, p - 1, c, flat, twice_diag)
            add_part(1, c, k_here)
            k_here, cz_before = k_after, cz_here

    def sweep(k, buf, write, sent=None):
        @pl.loop(0, steps)
        def _(i):
            p, order, edge = place_of(i)
            at = tiles(edge)
            flat = tuple(pl.multiple_of(t - TOP, 8) for t in at)
            if k == 2:
                pl.when(i == inner // 2)(pass_on)
            arrivals(i, (k,), sent)

            def here_at(c):
                return get(buf, p, c % chunks, at)

            q_before = get(cz, p - 1, chunks - 1, flat) * here_at(chunks - 1)
            here = here_at(0)
            for c in range(chunks):
                after = here_at(c + 1)
                cz_here = get(cz, p - 1, c, flat)
                q_here = cz_here * here
                total = (
                    (get(cx, p, c, flat) * get(buf, p + 1, c, at) + get(cx, p - 1, c, flat) * get(buf, p - 1, c, at))
                    + (
                        get(cy, p - 1, c, at) * get(buf, p, c, at, 1)
                        + get(cy, p - 1, c, at, -1) * get(buf, p, c, at, -1)
                    )
                ) + (cz_here * next_col(here, after) + prev_col(q_before, q_here))
                write(p, order, c, at, flat, here, total)
                here, q_before = after, q_here

            if k == 3:
                @pl.when((i >= inner) & (i < 2 * inner) & (lax.rem(i - inner, 4) == 3))
                def _():
                    store_planes(i - inner - 2, 4)

    def write_first(p, order, c, at, flat, here, total):
        twice_diag = get(wgt, p - 1, c, flat)
        resid = get(src, p - 1, c, flat) - 0.5 * (twice_diag * here - total)
        weight = damping / twice_diag
        first = (2.0 * weight) * resid
        put(wgt, p - 1, c, flat, weight)
        put(corr1, p, c, at, first)
        pack(2, order, c, first)
        add_part(0, c, resid)

    wait_load(2)
    sweep(1, prev, write_first, 2)
    start_all(plane_copies(2))
    start_all(row_copies(2, 1))

    lines = 2 * half * chunks
    sums = jnp.sum(acc[...], axis=1)
    per_chunk = LANES // F
    lane_row = lax.broadcasted_iota(jnp.int32, (LANES, LANES), 0)
    lane_col = lax.broadcasted_iota(jnp.int32, (LANES, LANES), 1)
    pool = jnp.where(lax.rem(lane_col, per_chunk) == lax.div(lane_row, F), 1.0, 0.0)
    pooled = jnp.dot(sums, pool, precision=HI, preferred_element_type=jnp.float32)
    line_row = lax.broadcasted_iota(jnp.int32, (lines, LANES), 0)
    line_col = lax.broadcasted_iota(jnp.int32, (lines, LANES), 1)
    pooled = jnp.where(lax.div(line_col, per_chunk) == lax.rem(line_row, chunks), pooled, 0.0)
    small = jnp.sum(pooled.reshape(2 * half, chunks, LANES), axis=1) * (1.0 / (F * F * F))
    part[gy, 0 : 2 * half, :] = small

    def part_copy(j):
        return pltpu.make_async_remote_copy(
            src_ref=part.at[gy], dst_ref=part.at[gy], send_sem=psend_sem.at[j], recv_sem=precv_sem.at[j],
            device_id=(gx, lax.rem(gy + j, ny)), device_id_type=MESH,
        )

    def part_arrival(j):
        at = lax.rem(gy + ny - j, ny)
        return pltpu.make_async_remote_copy(
            src_ref=part.at[at], dst_ref=part.at[at], send_sem=psend_sem.at[j], recv_sem=precv_sem.at[j],
            device_id=(gx, lax.rem(gy + j, ny)), device_id_type=MESH,
        )

    def gather_copy(j):
        return pltpu.make_async_remote_copy(
            src_ref=gather.at[gx], dst_ref=gather.at[gx], send_sem=gsend_sem.at[j], recv_sem=grecv_sem.at[j],
            device_id=(lax.rem(gx + j, nx), gy), device_id_type=MESH,
        )

    def gather_arrival(j):
        at = lax.rem(gx + nx - j, nx)
        return pltpu.make_async_remote_copy(
            src_ref=gather.at[at], dst_ref=gather.at[at], send_sem=gsend_sem.at[j], recv_sem=grecv_sem.at[j],
            device_id=(lax.rem(gx + j, nx), gy), device_id_type=MESH,
        )

    for j in range(1, ny):
        part_copy(j).start()

    def pass_on():
        for j in range(1, ny):
            part_arrival(j).wait_recv()
        for y in range(ny):
            for f in range(2):
                gather[gx, f, y * half : (y + 1) * half, :] = part[y, f * half : (f + 1) * half, :]
        for j in range(1, nx):
            gather_copy(j).start()

    def write_second(p, order, c, at, flat, here, total):
        second = (1.0 + (1.0 - damping)) * here + get(wgt, p - 1, c, flat) * total
        put(corr2, p, c, at, second)
        pack(3, order, c, second)

    sweep(2, corr1, write_second, 3)
    start_all(plane_copies(3))
    start_all(row_copies(3, 1))

    for j in range(1, nx):
        gather_arrival(j).wait_recv()
    crows = ny * half
    resid = gather[:, 0]
    ccond = gather[:, 1]

    def around(v):
        return (
            jnp.concatenate([v[1:], v[:1]], axis=0), jnp.concatenate([v[-1:], v[:-1]], axis=0),
            pltpu.roll(v, crows - 1, 1), pltpu.roll(v, 1, 1),
            pltpu.roll(v, 1, 2), pltpu.roll(v, LANES - 1, 2),
        )

    ccoup = [(0.5 * coarse_factor) * (ccond + near) for near in around(ccond)]
    cdiag = jnp.full_like(ccond, reaction)
    for one in ccoup:
        cdiag = cdiag + one
    cwgt = damping / cdiag
    ccoup = [cwgt * one for one in ccoup]
    cfirst = cwgt * resid

    def coarse_step(_, v):
        result = (1.0 - damping) * v + cfirst
        for one, near in zip(ccoup, around(v)):
            result = result + one * near
        return result

    coarse[...] = lax.fori_loop(0, CSWEEPS - 1, coarse_step, cfirst)
    turn = lax.rem(2 * crows + 1 - gy * half, crows)
    block = []
    for a in range(3):
        plane = coarse[lax.rem(gx + nx - 1 + a, nx)]
        block.append(pltpu.roll(plane, turn, 0)[0:8])
    block = jnp.concatenate(block, axis=0)
    ccols = chunks * LANES // F
    for c in range(chunks):
        fine = c * LANES + lane_col
        base = lax.div(fine, F)
        offset = (lax.rem(fine, F).astype(jnp.float32) + 0.5) / F - 0.5
        side = lax.rem(jnp.where(offset > 0, base + 1, base + ccols - 1), ccols)
        spread = jnp.where(lane_row == base, 1.0 - jnp.abs(offset), 0.0)
        spread = spread + jnp.where(lane_row == side, jnp.abs(offset), 0.0)
        cols_ref[:, c * LANES : (c + 1) * LANES] = jnp.dot(
            block, spread, precision=HI, preferred_element_type=jnp.float32
        )

    def out_copy(c, start, count):
        return pltpu.make_async_copy(
            src.at[pl.ds(start, count), c],
            out_hbm.at[pl.ds(start, count), :, pl.ds(c * LANES, LANES)],
            out_sem,
        )

    def store_planes(start, count):
        for c in range(chunks):
            out_copy(c, start, count).start()

    def write_third(p, order, c, at, flat, here, total):
        term = get(wgt, p - 1, c, flat) * total
        put(src, p - 1, c, flat, ((1.0 - damping) * here + get(corr1, p, c, at)) + term)

    sweep(3, corr2, write_third)
    store_planes(planes - 3, 3)
    store_planes(0, 1)

    for k in range(4):
        for copy in plane_copies(k) + row_copies(k, 0) + row_copies(k, 1):
            copy.wait_send()
    for j in range(1, ny):
        part_copy(j).wait_send()
    for j in range(1, nx):
        gather_copy(j).wait_send()
    pltpu.make_async_copy(src, src, out_sem).wait()


def add_kernel(step_planes, rows, fine_ref, cols_ref, out_ref, across):
    step = pl.program_id(0)
    half = rows // F

    @pl.when(step == 0)
    def _():
        row = lax.broadcasted_iota(jnp.int32, (rows, LANES), 0)
        base = lax.div(row, F) + 1
        offset = (lax.rem(row, F).astype(jnp.float32) + 0.5) / F - 0.5
        side = jnp.where(offset > 0, base + 1, base - 1)
        weights = [
            jnp.where(base == b, 1.0 - jnp.abs(offset), 0.0) + jnp.where(side == b, jnp.abs(offset), 0.0)
            for b in range(half + 2)
        ]
        for a in range(3):
            for c in range(cols_ref.shape[1] // LANES):
                at = pl.ds(c * LANES, LANES)
                total = weights[0] * cols_ref[8 * a : 8 * a + 1, at]
                for b in range(1, half + 2):
                    total = total + weights[b] * cols_ref[8 * a + b : 8 * a + b + 1, at]
                across[a, :, at] = total

    for q in range(step_planes):
        plane = step * step_planes + q
        offset = (plane.astype(jnp.float32) + 0.5) / F - 0.5
        side = jnp.where(offset > 0, 2, 0)
        weight = jnp.abs(offset)
        out_ref[q] = fine_ref[q] + ((1.0 - weight) * across[1] + weight * across[side])


def per_device(nx, ny, previous, source, conductivity):
    planes, rows, cols = previous.shape
    chunks = cols // LANES
    half = rows // F
    f32 = jnp.float32
    padded = pltpu.VMEM((planes + 2, chunks, rows + 16, LANES), f32)
    plain = pltpu.VMEM((planes, chunks, rows, LANES), f32)
    any_spec = pl.BlockSpec(memory_space=pl.ANY)
    fine, along = pl.pallas_call(
        functools.partial(main_kernel, nx, ny, planes, rows, chunks),
        out_shape=(
            jax.ShapeDtypeStruct((planes, rows, cols), f32),
            jax.ShapeDtypeStruct((24, cols), f32),
        ),
        in_specs=[any_spec] * 3,
        out_specs=(any_spec, pl.BlockSpec(memory_space=pltpu.VMEM)),
        scratch_shapes=[
            padded, padded, padded, padded, plain, plain,
            pltpu.VMEM((planes + 1, chunks, rows, LANES), f32),
            pltpu.VMEM((planes, chunks, rows + 8, LANES), f32),
            plain,
            pltpu.VMEM((4, 2, planes * chunks, LANES), f32),
            pltpu.VMEM((4, 2, planes * chunks, LANES), f32),
            pltpu.VMEM((2 * half * chunks, 8, LANES), f32),
            pltpu.VMEM((ny, 8, LANES), f32),
            pltpu.VMEM((nx, 2, ny * half, LANES), f32),
            pltpu.VMEM((nx, ny * half, LANES), f32),
            pltpu.SemaphoreType.DMA((3,)),
            pltpu.SemaphoreType.DMA,
            pltpu.SemaphoreType.DMA((32,)),
            pltpu.SemaphoreType.DMA((32,)),
            pltpu.SemaphoreType.DMA((ny,)),
            pltpu.SemaphoreType.DMA((ny,)),
            pltpu.SemaphoreType.DMA((nx,)),
            pltpu.SemaphoreType.DMA((nx,)),
        ],
        compiler_params=pltpu.CompilerParams(
            collective_id=0, has_side_effects=True, vmem_limit_bytes=58 * 1024 * 1024
        ),
        name="correction_main",
    )(previous, source, conductivity)
    step_planes = 4
    return pl.pallas_call(
        functools.partial(add_kernel, step_planes, rows),
        out_shape=jax.ShapeDtypeStruct((planes, rows, cols), f32),
        grid=(planes // step_planes,),
        in_specs=[
            pl.BlockSpec((step_planes, rows, cols), lambda i: (i, 0, 0)),
            pl.BlockSpec((24, cols), lambda i: (0, 0)),
        ],
        out_specs=pl.BlockSpec((step_planes, rows, cols), lambda i: (i, 0, 0)),
        scratch_shapes=[pltpu.VMEM((3, rows, cols), f32)],
        compiler_params=pltpu.CompilerParams(vmem_limit_bytes=60 * 1024 * 1024),
        name="interpolate_add",
    )(fine, along)


def solution(mesh):
    placed = P("gx", "gy", None)
    nx, ny = mesh.shape["gx"], mesh.shape["gy"]
    return jax.shard_map(
        functools.partial(per_device, nx, ny), mesh=mesh, in_specs=(placed,) * 3, out_specs=placed,
        check_vma=False,
    )
```

```python
import functools

import jax
import jax.numpy as jnp
from jax import lax
from jax.experimental import pallas as pl
from jax.experimental.pallas import tpu as pltpu
from jax.sharding import PartitionSpec as P

F = 16
CSWEEPS = 32
LANES = 128
TOP = 8

reaction = 0.2
damping = 0.8
coarse_factor = 0.25

MESH = pl.DeviceIdType.MESH
HI = lax.Precision.HIGHEST


def lane_index(shape):
    return lax.broadcasted_iota(jnp.int32, shape, len(shape) - 1)


def next_col(here, after):
    first = lane_index(here.shape) == 0
    return pltpu.roll(jnp.where(first, after, here), LANES - 1, 1)


def prev_col(before, here):
    last = lane_index(here.shape) == LANES - 1
    return pltpu.roll(jnp.where(last, before, here), 1, 1)


def main_kernel(
    nx, ny, planes, rows, chunks,
    prev_hbm, src_hbm, cond_hbm, out_hbm, cols_ref,
    cond, prev, corr1, corr2, src, wgt, cx, cy, cz,
    row_send, row_recv, acc, part, gather, coarse,
    load_sem, out_sem, send_sem, recv_sem, psend_sem, precv_sem, gsend_sem, grecv_sem,
):
    gx, gy = lax.axis_index("gx"), lax.axis_index("gy")
    body_rows = pl.ds(TOP, rows)
    last_row = TOP + rows - 1
    inner = planes - 2
    steps = 2 * planes

    def place_of(i):
        late = lax.div(i, 2 * inner)
        past = i - 2 * inner
        edge = (1 - late) * lax.div(i, inner) + late * lax.rem(past, 2)
        order = (1 - late) * lax.rem(i, inner) + late * (inner + lax.div(past, 2))
        return lax.rem(order + 1, planes) + 1, order, edge

    def tiles(edge):
        low = TOP + rows // 2 - 8 - (rows // 2 - 8) * edge
        high = TOP + rows // 2 + (rows // 2 - 8) * edge
        return pl.multiple_of(low, 8), pl.multiple_of(high, 8)

    def get(ref, p, c, at, shift=0):
        return jnp.concatenate([ref[p, c, pl.ds(t + shift, 8), :] for t in at], axis=0)

    def put(ref, p, c, at, block):
        ref[p, c, pl.ds(at[0], 8), :] = block[0:8]
        ref[p, c, pl.ds(at[1], 8), :] = block[8:16]

    loads = ((cond_hbm, cond, True), (prev_hbm, prev, True), (src_hbm, src, False))
    for k, (hbm, buf, padded) in enumerate(loads):
        for c in range(chunks):
            part_hbm = hbm.at[:, :, pl.ds(c * LANES, LANES)]
            dst = buf.at[pl.ds(1, planes), c, body_rows, :] if padded else buf.at[:, c]
            pltpu.make_async_copy(part_hbm, dst, load_sem.at[k]).start()

    def wait_load(k):
        pltpu.make_async_copy(src, src, load_sem.at[k]).wait()

    barrier = pltpu.get_barrier_semaphore()
    for j in range(1, nx):
        pl.semaphore_signal(barrier, inc=1, device_id=(lax.rem(gx + j, nx), gy), device_id_type=MESH)
    for j in range(1, ny):
        pl.semaphore_signal(barrier, inc=1, device_id=(gx, lax.rem(gy + j, ny)), device_id_type=MESH)
    pl.semaphore_wait(barrier, nx + ny - 2)

    x_next, x_prev = (lax.rem(gx + 1, nx), gy), (lax.rem(gx + nx - 1, nx), gy)
    y_next, y_prev = (gx, lax.rem(gy + 1, ny)), (gx, lax.rem(gy + ny - 1, ny))
    fields = (cond, prev, corr1, corr2)

    def remote(source, target, sem, device):
        return pltpu.make_async_remote_copy(
            src_ref=source, dst_ref=target, send_sem=send_sem.at[sem], recv_sem=recv_sem.at[sem],
            device_id=device, device_id_type=MESH,
        )

    def plane_copies(k):
        buf = fields[k]
        return (
            remote(buf.at[1, :, body_rows, :], buf.at[planes + 1, :, body_rows, :], 2 * k, x_prev),
            remote(buf.at[planes, :, body_rows, :], buf.at[0, :, body_rows, :], 2 * k + 1, x_next),
        )

    cut = inner * chunks

    def row_copies(k, late):
        lines = pl.ds(cut, 2 * chunks) if late else pl.ds(0, cut)
        sem = 16 + 4 * k + 2 * late
        return (
            remote(row_send.at[k, 0, lines], row_recv.at[k, 0, lines], sem, y_prev),
            remote(row_send.at[k, 1, lines], row_recv.at[k, 1, lines], sem + 1, y_next),
        )

    def start_all(copies):
        for copy in copies:
            copy.start()

    def wait_recv(copies):
        for copy in copies:
            copy.wait_recv()

    def pack(k, order, c, block):
        at = order * chunks + c
        row_send[k, 0, pl.ds(at, 1), :] = block[0:1]
        row_send[k, 1, pl.ds(at, 1), :] = block[15:16]

    def pack_all(k):
        buf = fields[k]

        @pl.loop(0, planes)
        def _(order):
            p = lax.rem(order + 1, planes) + 1
            for c in range(chunks):
                at = order * chunks + c
                row_send[k, 0, pl.ds(at, 1), :] = buf[p, c, TOP : TOP + 1, :]
                row_send[k, 1, pl.ds(at, 1), :] = buf[p, c, last_row : last_row + 1, :]

    def unpack(k, first, last):
        buf = fields[k]

        @pl.loop(first, last)
        def _(order):
            p = lax.rem(order + 1, planes) + 1
            for c in range(chunks):
                at = order * chunks + c
                buf[p, c, last_row + 1 : last_row + 2, :] = row_recv[k, 0, pl.ds(at, 1), :]
                buf[p, c, TOP - 1 : TOP, :] = row_recv[k, 1, pl.ds(at, 1), :]

    def arrivals(i, ks, sent=None):
        @pl.when(i == inner)
        def _():
            for k in ks:
                wait_recv(row_copies(k, 0))
                unpack(k, 0, inner)

        @pl.when(i == 2 * inner)
        def _():
            if sent is not None:
                start_all(row_copies(sent, 0))
            for k in ks:
                wait_recv(row_copies(k, 1))
                unpack(k, inner, planes)
                wait_recv(plane_copies(k))

    for k in (0, 1):
        wait_load(k)
        start_all(plane_copies(k))
        pack_all(k)
        start_all(row_copies(k, 0))
        start_all(row_copies(k, 1))
    acc[...] = jnp.zeros_like(acc)

    half = rows // F

    def add_part(field, c, block):
        for r in range(half):
            at = (field * half + r) * chunks + c
            acc[at] = acc[at] + block[8 * r : 8 * r + 8]

    @pl.loop(0, steps)
    def _(i):
        p, order, edge = place_of(i)
        at = tiles(edge)
        flat = tuple(pl.multiple_of(t - TOP, 8) for t in at)
        arrivals(i, (0,))

        def cond_at(c):
            return get(cond, p, c % chunks, at)

        ready = []
        k_here = cond_at(chunks - 1)
        k_after = cond_at(0)
        cz_before = k_here + next_col(k_here, k_after)
        k_here = k_after
        for c in range(chunks):
            k_after = cond_at(c + 1)
            cz_here = k_here + next_col(k_here, k_after)
            cz_low = prev_col(cz_before, cz_here)
            cx_high = k_here + get(cond, p + 1, c, at)
            cx_low = k_here + get(cond, p - 1, c, at)
            cy_high = k_here + get(cond, p, c, at, 1)
            cy_low = k_here + get(cond, p, c, at, -1)
            twice_diag = (((cx_high + cx_low) + (cy_high + cy_low)) + (cz_here + cz_low)) + 2 * reaction
            ready.append((c, cz_here, cx_high, cx_low, cy_high, cy_low[0:1], twice_diag, k_here))
            k_here, cz_before = k_after, cz_here
            if len(ready) == 4:
                for d, c_z, c_xh, c_xl, c_yh, c_yl, twice, kept in ready:
                    put(cz, p - 1, d, flat, c_z)
                    put(cx, p, d, flat, c_xh)
                    put(cx, p - 1, d, flat, c_xl)
                    put(cy, p - 1, d, at, c_yh)
                    cy[p - 1, d, pl.ds(at[0] - 1, 1), :] = c_yl
                    put(wgt, p - 1, d, flat, twice)
                    add_part(1, d, kept)
                ready = []

    def sweep(k, buf, make, write, group, sent=None):
        @pl.loop(0, steps)
        def _(i):
            p, order, edge = place_of(i)
            at = tiles(edge)
            flat = tuple(pl.multiple_of(t - TOP, 8) for t in at)
            if k == 2:
                pl.when(i == inner // 2)(pass_on)
            arrivals(i, (k,), sent)

            def here_at(c):
                return get(buf, p, c % chunks, at)

            ready = []
            q_before = get(cz, p - 1, chunks - 1, flat) * here_at(chunks - 1)
            here = here_at(0)
            for c in range(chunks):
                after = here_at(c + 1)
                cz_here = get(cz, p - 1, c, flat)
                q_here = cz_here * here
                total = (
                    (get(cx, p, c, flat) * get(buf, p + 1, c, at) + get(cx, p - 1, c, flat) * get(buf, p - 1, c, at))
                    + (
                        get(cy, p - 1, c, at) * get(buf, p, c, at, 1)
                        + get(cy, p - 1, c, at, -1) * get(buf, p, c, at, -1)
                    )
                ) + (cz_here * next_col(here, after) + prev_col(q_before, q_here))
                ready.append((c, make(p, c, at, flat, here, total)))
                here, q_before = after, q_here
                if len(ready) == group:
                    for d, made in ready:
                        write(p, order, d, at, flat, *made)
                    ready = []

            if k == 3:
                @pl.when((i >= inner) & (i < 2 * inner) & (lax.rem(i - inner, 4) == 3))
                def _():
                    store_planes(i - inner - 2, 4)

    def make_first(p, c, at, flat, here, total):
        twice_diag = get(wgt, p - 1, c, flat)
        resid = get(src, p - 1, c, flat) - 0.5 * (twice_diag * here - total)
        weight = damping / twice_diag
        return weight, (2.0 * weight) * resid, resid

    def write_first(p, order, c, at, flat, weight, first, resid):
        put(wgt, p - 1, c, flat, weight)
        put(corr1, p, c, at, first)
        pack(2, order, c, first)
        add_part(0, c, resid)

    wait_load(2)
    sweep(1, prev, make_first, write_first, 4, 2)
    start_all(plane_copies(2))
    start_all(row_copies(2, 1))

    lines = 2 * half * chunks
    sums = jnp.sum(acc[...], axis=1)
    per_chunk = LANES // F
    lane_row = lax.broadcasted_iota(jnp.int32, (LANES, LANES), 0)
    lane_col = lax.broadcasted_iota(jnp.int32, (LANES, LANES), 1)
    pool = jnp.where(lax.rem(lane_col, per_chunk) == lax.div(lane_row, F), 1.0, 0.0)
    pooled = jnp.dot(sums, pool, precision=HI, preferred_element_type=jnp.float32)
    line_row = lax.broadcasted_iota(jnp.int32, (lines, LANES), 0)
    line_col = lax.broadcasted_iota(jnp.int32, (lines, LANES), 1)
    pooled = jnp.where(lax.div(line_col, per_chunk) == lax.rem(line_row, chunks), pooled, 0.0)
    small = jnp.sum(pooled.reshape(2 * half, chunks, LANES), axis=1) * (1.0 / (F * F * F))
    part[gy, 0 : 2 * half, :] = small

    def part_copy(j):
        return pltpu.make_async_remote_copy(
            src_ref=part.at[gy], dst_ref=part.at[gy], send_sem=psend_sem.at[j], recv_sem=precv_sem.at[j],
            device_id=(gx, lax.rem(gy + j, ny)), device_id_type=MESH,
        )

    def part_arrival(j):
        at = lax.rem(gy + ny - j, ny)
        return pltpu.make_async_remote_copy(
            src_ref=part.at[at], dst_ref=part.at[at], send_sem=psend_sem.at[j], recv_sem=precv_sem.at[j],
            device_id=(gx, lax.rem(gy + j, ny)), device_id_type=MESH,
        )

    def gather_copy(j):
        return pltpu.make_async_remote_copy(
            src_ref=gather.at[gx], dst_ref=gather.at[gx], send_sem=gsend_sem.at[j], recv_sem=grecv_sem.at[j],
            device_id=(lax.rem(gx + j, nx), gy), device_id_type=MESH,
        )

    def gather_arrival(j):
        at = lax.rem(gx + nx - j, nx)
        return pltpu.make_async_remote_copy(
            src_ref=gather.at[at], dst_ref=gather.at[at], send_sem=gsend_sem.at[j], recv_sem=grecv_sem.at[j],
            device_id=(lax.rem(gx + j, nx), gy), device_id_type=MESH,
        )

    for j in range(1, ny):
        part_copy(j).start()

    def pass_on():
        for j in range(1, ny):
            part_arrival(j).wait_recv()
        for y in range(ny):
            for f in range(2):
                gather[gx, f, y * half : (y + 1) * half, :] = part[y, f * half : (f + 1) * half, :]
        for j in range(1, nx):
            gather_copy(j).start()

    def make_second(p, c, at, flat, here, total):
        return ((1.0 + (1.0 - damping)) * here + get(wgt, p - 1, c, flat) * total,)

    def write_second(p, order, c, at, flat, second):
        put(corr2, p, c, at, second)
        pack(3, order, c, second)

    sweep(2, corr1, make_second, write_second, 8, 3)
    start_all(plane_copies(3))
    start_all(row_copies(3, 1))

    for j in range(1, nx):
        gather_arrival(j).wait_recv()
    crows = ny * half
    resid = gather[:, 0]
    ccond = gather[:, 1]

    def around(v):
        return (
            jnp.concatenate([v[1:], v[:1]], axis=0), jnp.concatenate([v[-1:], v[:-1]], axis=0),
            pltpu.roll(v, crows - 1, 1), pltpu.roll(v, 1, 1),
            pltpu.roll(v, 1, 2), pltpu.roll(v, LANES - 1, 2),
        )

    ccoup = [(0.5 * coarse_factor) * (ccond + near) for near in around(ccond)]
    cdiag = jnp.full_like(ccond, reaction)
    for one in ccoup:
        cdiag = cdiag + one
    cwgt = damping / cdiag
    ccoup = [cwgt * one for one in ccoup]
    cfirst = cwgt * resid

    def coarse_step(_, v):
        result = (1.0 - damping) * v + cfirst
        for one, near in zip(ccoup, around(v)):
            result = result + one * near
        return result

    coarse[...] = lax.fori_loop(0, CSWEEPS - 1, coarse_step, cfirst)
    turn = lax.rem(2 * crows + 1 - gy * half, crows)
    block = []
    for a in range(3):
        plane = coarse[lax.rem(gx + nx - 1 + a, nx)]
        block.append(pltpu.roll(plane, turn, 0)[0:8])
    block = jnp.concatenate(block, axis=0)
    ccols = chunks * LANES // F
    for c in range(chunks):
        fine = c * LANES + lane_col
        base = lax.div(fine, F)
        offset = (lax.rem(fine, F).astype(jnp.float32) + 0.5) / F - 0.5
        side = lax.rem(jnp.where(offset > 0, base + 1, base + ccols - 1), ccols)
        spread = jnp.where(lane_row == base, 1.0 - jnp.abs(offset), 0.0)
        spread = spread + jnp.where(lane_row == side, jnp.abs(offset), 0.0)
        cols_ref[:, c * LANES : (c + 1) * LANES] = jnp.dot(
            block, spread, precision=HI, preferred_element_type=jnp.float32
        )

    def out_copy(c, start, count):
        return pltpu.make_async_copy(
            src.at[pl.ds(start, count), c],
            out_hbm.at[pl.ds(start, count), :, pl.ds(c * LANES, LANES)],
            out_sem,
        )

    def store_planes(start, count):
        for c in range(chunks):
            out_copy(c, start, count).start()

    def make_third(p, c, at, flat, here, total):
        term = get(wgt, p - 1, c, flat) * total
        return (((1.0 - damping) * here + get(corr1, p, c, at)) + term,)

    def write_third(p, order, c, at, flat, third):
        put(src, p - 1, c, flat, third)

    sweep(3, corr2, make_third, write_third, 8)
    store_planes(planes - 3, 3)
    store_planes(0, 1)

    for k in range(4):
        for copy in plane_copies(k) + row_copies(k, 0) + row_copies(k, 1):
            copy.wait_send()
    for j in range(1, ny):
        part_copy(j).wait_send()
    for j in range(1, nx):
        gather_copy(j).wait_send()
    pltpu.make_async_copy(src, src, out_sem).wait()


def add_kernel(step_planes, rows, fine_ref, cols_ref, out_ref, across):
    step = pl.program_id(0)
    half = rows // F

    @pl.when(step == 0)
    def _():
        row = lax.broadcasted_iota(jnp.int32, (rows, LANES), 0)
        base = lax.div(row, F) + 1
        offset = (lax.rem(row, F).astype(jnp.float32) + 0.5) / F - 0.5
        side = jnp.where(offset > 0, base + 1, base - 1)
        weights = [
            jnp.where(base == b, 1.0 - jnp.abs(offset), 0.0) + jnp.where(side == b, jnp.abs(offset), 0.0)
            for b in range(half + 2)
        ]
        for a in range(3):
            for c in range(cols_ref.shape[1] // LANES):
                at = pl.ds(c * LANES, LANES)
                total = weights[0] * cols_ref[8 * a : 8 * a + 1, at]
                for b in range(1, half + 2):
                    total = total + weights[b] * cols_ref[8 * a + b : 8 * a + b + 1, at]
                across[a, :, at] = total

    for q in range(step_planes):
        plane = step * step_planes + q
        offset = (plane.astype(jnp.float32) + 0.5) / F - 0.5
        side = jnp.where(offset > 0, 2, 0)
        weight = jnp.abs(offset)
        out_ref[q] = fine_ref[q] + ((1.0 - weight) * across[1] + weight * across[side])


def per_device(nx, ny, previous, source, conductivity):
    planes, rows, cols = previous.shape
    chunks = cols // LANES
    half = rows // F
    f32 = jnp.float32
    padded = pltpu.VMEM((planes + 2, chunks, rows + 16, LANES), f32)
    plain = pltpu.VMEM((planes, chunks, rows, LANES), f32)
    any_spec = pl.BlockSpec(memory_space=pl.ANY)
    fine, along = pl.pallas_call(
        functools.partial(main_kernel, nx, ny, planes, rows, chunks),
        out_shape=(
            jax.ShapeDtypeStruct((planes, rows, cols), f32),
            jax.ShapeDtypeStruct((24, cols), f32),
        ),
        in_specs=[any_spec] * 3,
        out_specs=(any_spec, pl.BlockSpec(memory_space=pltpu.VMEM)),
        scratch_shapes=[
            padded, padded, padded, padded, plain, plain,
            pltpu.VMEM((planes + 1, chunks, rows, LANES), f32),
            pltpu.VMEM((planes, chunks, rows + 8, LANES), f32),
            plain,
            pltpu.VMEM((4, 2, planes * chunks, LANES), f32),
            pltpu.VMEM((4, 2, planes * chunks, LANES), f32),
            pltpu.VMEM((2 * half * chunks, 8, LANES), f32),
            pltpu.VMEM((ny, 8, LANES), f32),
            pltpu.VMEM((nx, 2, ny * half, LANES), f32),
            pltpu.VMEM((nx, ny * half, LANES), f32),
            pltpu.SemaphoreType.DMA((3,)),
            pltpu.SemaphoreType.DMA,
            pltpu.SemaphoreType.DMA((32,)),
            pltpu.SemaphoreType.DMA((32,)),
            pltpu.SemaphoreType.DMA((ny,)),
            pltpu.SemaphoreType.DMA((ny,)),
            pltpu.SemaphoreType.DMA((nx,)),
            pltpu.SemaphoreType.DMA((nx,)),
        ],
        compiler_params=pltpu.CompilerParams(
            collective_id=0, has_side_effects=True, vmem_limit_bytes=58 * 1024 * 1024
        ),
        name="correction_main",
    )(previous, source, conductivity)
    step_planes = 4
    return pl.pallas_call(
        functools.partial(add_kernel, step_planes, rows),
        out_shape=jax.ShapeDtypeStruct((planes, rows, cols), f32),
        grid=(planes // step_planes,),
        in_specs=[
            pl.BlockSpec((step_planes, rows, cols), lambda i: (i, 0, 0)),
            pl.BlockSpec((24, cols), lambda i: (0, 0)),
        ],
        out_specs=pl.BlockSpec((step_planes, rows, cols), lambda i: (i, 0, 0)),
        scratch_shapes=[pltpu.VMEM((3, rows, cols), f32)],
        compiler_params=pltpu.CompilerParams(vmem_limit_bytes=60 * 1024 * 1024),
        name="interpolate_add",
    )(fine, along)


def solution(mesh):
    placed = P("gx", "gy", None)
    nx, ny = mesh.shape["gx"], mesh.shape["gy"]
    return jax.shard_map(
        functools.partial(per_device, nx, ny), mesh=mesh, in_specs=(placed,) * 3, out_specs=placed,
        check_vma=False,
    )
```

```python
import functools

import jax
import jax.numpy as jnp
from jax import lax
from jax.experimental import pallas as pl
from jax.experimental.pallas import tpu as pltpu
from jax.sharding import PartitionSpec as P

F = 16
CSWEEPS = 32
LANES = 128
TOP = 8

reaction = 0.2
damping = 0.8
coarse_factor = 0.25

MESH = pl.DeviceIdType.MESH
HI = lax.Precision.HIGHEST


def lane_index(shape):
    return lax.broadcasted_iota(jnp.int32, shape, len(shape) - 1)


def next_col(here, after):
    first = lane_index(here.shape) == 0
    return pltpu.roll(jnp.where(first, after, here), LANES - 1, 1)


def prev_col(before, here):
    last = lane_index(here.shape) == LANES - 1
    return pltpu.roll(jnp.where(last, before, here), 1, 1)


def main_kernel(
    nx, ny, planes, rows, chunks,
    prev_hbm, src_hbm, cond_hbm, out_hbm, cols_ref,
    cond, prev, corr1, corr2, src, wgt, cx, cy, cz,
    acc, part, gather, coarse,
    load_sem, out_sem, send_sem, recv_sem, psend_sem, precv_sem, gsend_sem, grecv_sem,
):
    gx, gy = lax.axis_index("gx"), lax.axis_index("gy")
    body_rows = pl.ds(TOP, rows)
    last_row = TOP + rows - 1
    inner = planes - 2
    steps = 2 * planes

    def place_of(i):
        late = lax.div(i, 2 * inner)
        past = i - 2 * inner
        edge = (1 - late) * lax.div(i, inner) + late * lax.rem(past, 2)
        order = (1 - late) * lax.rem(i, inner) + late * (inner + lax.div(past, 2))
        return lax.rem(order + 1, planes) + 1, order, edge

    def tiles(edge):
        low = TOP + rows // 2 - 8 - (rows // 2 - 8) * edge
        high = TOP + rows // 2 + (rows // 2 - 8) * edge
        return pl.multiple_of(low, 8), pl.multiple_of(high, 8)

    def get(ref, p, c, at, shift=0):
        return jnp.concatenate([ref[p, c, pl.ds(t + shift, 8), :] for t in at], axis=0)

    def put(ref, p, c, at, block):
        ref[p, c, pl.ds(at[0], 8), :] = block[0:8]
        ref[p, c, pl.ds(at[1], 8), :] = block[8:16]

    loads = ((cond_hbm, cond, True), (prev_hbm, prev, True), (src_hbm, src, False))
    for k, (hbm, buf, padded) in enumerate(loads):
        for c in range(chunks):
            part_hbm = hbm.at[:, :, pl.ds(c * LANES, LANES)]
            dst = buf.at[pl.ds(1, planes), c, body_rows, :] if padded else buf.at[:, c]
            pltpu.make_async_copy(part_hbm, dst, load_sem.at[k]).start()

    def wait_load(k):
        pltpu.make_async_copy(src, src, load_sem.at[k]).wait()

    barrier = pltpu.get_barrier_semaphore()
    for j in range(1, nx):
        pl.semaphore_signal(barrier, inc=1, device_id=(lax.rem(gx + j, nx), gy), device_id_type=MESH)
    for j in range(1, ny):
        pl.semaphore_signal(barrier, inc=1, device_id=(gx, lax.rem(gy + j, ny)), device_id_type=MESH)
    pl.semaphore_wait(barrier, nx + ny - 2)

    x_next, x_prev = (lax.rem(gx + 1, nx), gy), (lax.rem(gx + nx - 1, nx), gy)
    y_next, y_prev = (gx, lax.rem(gy + 1, ny)), (gx, lax.rem(gy + ny - 1, ny))
    fields = (cond, prev, corr1, corr2)

    def remote(source, target, sem, device):
        return pltpu.make_async_remote_copy(
            src_ref=source, dst_ref=target, send_sem=send_sem.at[sem], recv_sem=recv_sem.at[sem],
            device_id=device, device_id_type=MESH,
        )

    def plane_copies(k):
        buf = fields[k]
        return (
            remote(buf.at[1, :, body_rows, :], buf.at[planes + 1, :, body_rows, :], 2 * k, x_prev),
            remote(buf.at[planes, :, body_rows, :], buf.at[0, :, body_rows, :], 2 * k + 1, x_next),
        )

    def row_copies(k, late):
        buf, copies = fields[k], []
        groups = ((1, 1), (planes, 1)) if late else ((2, inner),)
        for g, (first, count) in enumerate(groups):
            sem = 8 + 6 * k + (2 + 2 * g if late else 0)
            span = pl.ds(first, count)

            def row(at):
                return buf.at[span, :, pl.ds(at, 1), :]

            copies.append(remote(row(TOP), row(last_row + 1), sem, y_prev))
            copies.append(remote(row(last_row), row(TOP - 1), sem + 1, y_next))
        return tuple(copies)

    def start_all(copies):
        for copy in copies:
            copy.start()

    def wait_recv(copies):
        for copy in copies:
            copy.wait_recv()

    def arrivals(i, ks, sent=None):
        @pl.when(i == inner)
        def _():
            for k in ks:
                wait_recv(row_copies(k, 0))

        @pl.when(i == 2 * inner)
        def _():
            if sent is not None:
                start_all(row_copies(sent, 0))
            for k in ks:
                wait_recv(row_copies(k, 1))
                wait_recv(plane_copies(k))

    for k in (0, 1):
        wait_load(k)
        start_all(plane_copies(k))
        start_all(row_copies(k, 0))
        start_all(row_copies(k, 1))
    acc[...] = jnp.zeros_like(acc)

    half = rows // F

    def add_part(field, c, block):
        for r in range(half):
            at = (field * half + r) * chunks + c
            acc[at] = acc[at] + block[8 * r : 8 * r + 8]

    @pl.loop(0, steps)
    def _(i):
        p, order, edge = place_of(i)
        at = tiles(edge)
        flat = tuple(pl.multiple_of(t - TOP, 8) for t in at)
        arrivals(i, (0,))

        def cond_at(c):
            return get(cond, p, c % chunks, at)

        ready = []
        k_here = cond_at(chunks - 1)
        k_after = cond_at(0)
        cz_before = k_here + next_col(k_here, k_after)
        k_here = k_after
        for c in range(chunks):
            k_after = cond_at(c + 1)
            cz_here = k_here + next_col(k_here, k_after)
            cz_low = prev_col(cz_before, cz_here)
            cx_high = k_here + get(cond, p + 1, c, at)
            cx_low = k_here + get(cond, p - 1, c, at)
            cy_high = k_here + get(cond, p, c, at, 1)
            cy_low = k_here + get(cond, p, c, at, -1)
            twice_diag = (((cx_high + cx_low) + (cy_high + cy_low)) + (cz_here + cz_low)) + 2 * reaction
            ready.append((c, cz_here, cx_high, cx_low, cy_high, cy_low[0:1], twice_diag, k_here))
            k_here, cz_before = k_after, cz_here
            if len(ready) == 4:
                for d, c_z, c_xh, c_xl, c_yh, c_yl, twice, kept in ready:
                    put(cz, p - 1, d, flat, c_z)
                    put(cx, p, d, flat, c_xh)
                    put(cx, p - 1, d, flat, c_xl)
                    put(cy, p - 1, d, at, c_yh)
                    cy[p - 1, d, pl.ds(at[0] - 1, 1), :] = c_yl
                    put(wgt, p - 1, d, flat, twice)
                    add_part(1, d, kept)
                ready = []

    def sweep(k, buf, make, write, group, sent=None):
        @pl.loop(0, steps)
        def _(i):
            p, order, edge = place_of(i)
            at = tiles(edge)
            flat = tuple(pl.multiple_of(t - TOP, 8) for t in at)
            if k == 2:
                pl.when(i == inner // 2)(pass_on)
            arrivals(i, (k,), sent)

            def here_at(c):
                return get(buf, p, c % chunks, at)

            ready = []
            q_before = get(cz, p - 1, chunks - 1, flat) * here_at(chunks - 1)
            here = here_at(0)
            for c in range(chunks):
                after = here_at(c + 1)
                cz_here = get(cz, p - 1, c, flat)
                q_here = cz_here * here
                total = (
                    (get(cx, p, c, flat) * get(buf, p + 1, c, at) + get(cx, p - 1, c, flat) * get(buf, p - 1, c, at))
                    + (
                        get(cy, p - 1, c, at) * get(buf, p, c, at, 1)
                        + get(cy, p - 1, c, at, -1) * get(buf, p, c, at, -1)
                    )
                ) + (cz_here * next_col(here, after) + prev_col(q_before, q_here))
                ready.append((c, make(p, c, at, flat, here, total)))
                here, q_before = after, q_here
                if len(ready) == group:
                    for d, made in ready:
                        write(p, order, d, at, flat, *made)
                    ready = []

            if k == 3:
                @pl.when((i >= inner) & (i < 2 * inner) & (lax.rem(i - inner, 4) == 3))
                def _():
                    store_planes(i - inner - 2, 4)

    def make_first(p, c, at, flat, here, total):
        twice_diag = get(wgt, p - 1, c, flat)
        resid = get(src, p - 1, c, flat) - 0.5 * (twice_diag * here - total)
        weight = damping / twice_diag
        return weight, (2.0 * weight) * resid, resid

    def write_first(p, order, c, at, flat, weight, first, resid):
        put(wgt, p - 1, c, flat, weight)
        put(corr1, p, c, at, first)
        add_part(0, c, resid)

    wait_load(2)
    sweep(1, prev, make_first, write_first, 4, 2)
    start_all(plane_copies(2))
    start_all(row_copies(2, 1))

    lines = 2 * half * chunks
    sums = jnp.sum(acc[...], axis=1)
    per_chunk = LANES // F
    lane_row = lax.broadcasted_iota(jnp.int32, (LANES, LANES), 0)
    lane_col = lax.broadcasted_iota(jnp.int32, (LANES, LANES), 1)
    pool = jnp.where(lax.rem(lane_col, per_chunk) == lax.div(lane_row, F), 1.0, 0.0)
    pooled = jnp.dot(sums, pool, precision=HI, preferred_element_type=jnp.float32)
    line_row = lax.broadcasted_iota(jnp.int32, (lines, LANES), 0)
    line_col = lax.broadcasted_iota(jnp.int32, (lines, LANES), 1)
    pooled = jnp.where(lax.div(line_col, per_chunk) == lax.rem(line_row, chunks), pooled, 0.0)
    small = jnp.sum(pooled.reshape(2 * half, chunks, LANES), axis=1) * (1.0 / (F * F * F))
    part[gy, 0 : 2 * half, :] = small

    def part_copy(j):
        return pltpu.make_async_remote_copy(
            src_ref=part.at[gy], dst_ref=part.at[gy], send_sem=psend_sem.at[j], recv_sem=precv_sem.at[j],
            device_id=(gx, lax.rem(gy + j, ny)), device_id_type=MESH,
        )

    def part_arrival(j):
        at = lax.rem(gy + ny - j, ny)
        return pltpu.make_async_remote_copy(
            src_ref=part.at[at], dst_ref=part.at[at], send_sem=psend_sem.at[j], recv_sem=precv_sem.at[j],
            device_id=(gx, lax.rem(gy + j, ny)), device_id_type=MESH,
        )

    def gather_copy(j):
        return pltpu.make_async_remote_copy(
            src_ref=gather.at[gx], dst_ref=gather.at[gx], send_sem=gsend_sem.at[j], recv_sem=grecv_sem.at[j],
            device_id=(lax.rem(gx + j, nx), gy), device_id_type=MESH,
        )

    def gather_arrival(j):
        at = lax.rem(gx + nx - j, nx)
        return pltpu.make_async_remote_copy(
            src_ref=gather.at[at], dst_ref=gather.at[at], send_sem=gsend_sem.at[j], recv_sem=grecv_sem.at[j],
            device_id=(lax.rem(gx + j, nx), gy), device_id_type=MESH,
        )

    for j in range(1, ny):
        part_copy(j).start()

    def pass_on():
        for j in range(1, ny):
            part_arrival(j).wait_recv()
        for y in range(ny):
            for f in range(2):
                gather[gx, f, y * half : (y + 1) * half, :] = part[y, f * half : (f + 1) * half, :]
        for j in range(1, nx):
            gather_copy(j).start()

    def make_second(p, c, at, flat, here, total):
        return ((1.0 + (1.0 - damping)) * here + get(wgt, p - 1, c, flat) * total,)

    def write_second(p, order, c, at, flat, second):
        put(corr2, p, c, at, second)

    sweep(2, corr1, make_second, write_second, 8, 3)
    start_all(plane_copies(3))
    start_all(row_copies(3, 1))

    for j in range(1, nx):
        gather_arrival(j).wait_recv()
    crows = ny * half
    resid = gather[:, 0]
    ccond = gather[:, 1]

    def around(v):
        return (
            jnp.concatenate([v[1:], v[:1]], axis=0), jnp.concatenate([v[-1:], v[:-1]], axis=0),
            pltpu.roll(v, crows - 1, 1), pltpu.roll(v, 1, 1),
            pltpu.roll(v, 1, 2), pltpu.roll(v, LANES - 1, 2),
        )

    ccoup = [(0.5 * coarse_factor) * (ccond + near) for near in around(ccond)]
    cdiag = jnp.full_like(ccond, reaction)
    for one in ccoup:
        cdiag = cdiag + one
    cwgt = damping / cdiag
    ccoup = [cwgt * one for one in ccoup]
    cfirst = cwgt * resid

    def coarse_step(_, v):
        result = (1.0 - damping) * v + cfirst
        for one, near in zip(ccoup, around(v)):
            result = result + one * near
        return result

    coarse[...] = lax.fori_loop(0, CSWEEPS - 1, coarse_step, cfirst)
    turn = lax.rem(2 * crows + 1 - gy * half, crows)
    block = []
    for a in range(3):
        plane = coarse[lax.rem(gx + nx - 1 + a, nx)]
        block.append(pltpu.roll(plane, turn, 0)[0:8])
    block = jnp.concatenate(block, axis=0)
    ccols = chunks * LANES // F
    for c in range(chunks):
        fine = c * LANES + lane_col
        base = lax.div(fine, F)
        offset = (lax.rem(fine, F).astype(jnp.float32) + 0.5) / F - 0.5
        side = lax.rem(jnp.where(offset > 0, base + 1, base + ccols - 1), ccols)
        spread = jnp.where(lane_row == base, 1.0 - jnp.abs(offset), 0.0)
        spread = spread + jnp.where(lane_row == side, jnp.abs(offset), 0.0)
        cols_ref[:, c * LANES : (c + 1) * LANES] = jnp.dot(
            block, spread, precision=HI, preferred_element_type=jnp.float32
        )

    def out_copy(c, start, count):
        return pltpu.make_async_copy(
            src.at[pl.ds(start, count), c],
            out_hbm.at[pl.ds(start, count), :, pl.ds(c * LANES, LANES)],
            out_sem,
        )

    def store_planes(start, count):
        for c in range(chunks):
            out_copy(c, start, count).start()

    def make_third(p, c, at, flat, here, total):
        term = get(wgt, p - 1, c, flat) * total
        return (((1.0 - damping) * here + get(corr1, p, c, at)) + term,)

    def write_third(p, order, c, at, flat, third):
        put(src, p - 1, c, flat, third)

    sweep(3, corr2, make_third, write_third, 8)
    store_planes(planes - 3, 3)
    store_planes(0, 1)

    for k in range(4):
        for copy in plane_copies(k) + row_copies(k, 0) + row_copies(k, 1):
            copy.wait_send()
    for j in range(1, ny):
        part_copy(j).wait_send()
    for j in range(1, nx):
        gather_copy(j).wait_send()
    pltpu.make_async_copy(src, src, out_sem).wait()


def add_kernel(step_planes, rows, fine_ref, cols_ref, out_ref, across):
    step = pl.program_id(0)
    half = rows // F

    @pl.when(step == 0)
    def _():
        row = lax.broadcasted_iota(jnp.int32, (rows, LANES), 0)
        base = lax.div(row, F) + 1
        offset = (lax.rem(row, F).astype(jnp.float32) + 0.5) / F - 0.5
        side = jnp.where(offset > 0, base + 1, base - 1)
        weights = [
            jnp.where(base == b, 1.0 - jnp.abs(offset), 0.0) + jnp.where(side == b, jnp.abs(offset), 0.0)
            for b in range(half + 2)
        ]
        for a in range(3):
            for c in range(cols_ref.shape[1] // LANES):
                at = pl.ds(c * LANES, LANES)
                total = weights[0] * cols_ref[8 * a : 8 * a + 1, at]
                for b in range(1, half + 2):
                    total = total + weights[b] * cols_ref[8 * a + b : 8 * a + b + 1, at]
                across[a, :, at] = total

    for q in range(step_planes):
        plane = step * step_planes + q
        offset = (plane.astype(jnp.float32) + 0.5) / F - 0.5
        side = jnp.where(offset > 0, 2, 0)
        weight = jnp.abs(offset)
        out_ref[q] = fine_ref[q] + ((1.0 - weight) * across[1] + weight * across[side])


def per_device(nx, ny, previous, source, conductivity):
    planes, rows, cols = previous.shape
    chunks = cols // LANES
    half = rows // F
    f32 = jnp.float32
    padded = pltpu.VMEM((planes + 2, chunks, rows + 16, LANES), f32)
    plain = pltpu.VMEM((planes, chunks, rows, LANES), f32)
    any_spec = pl.BlockSpec(memory_space=pl.ANY)
    fine, along = pl.pallas_call(
        functools.partial(main_kernel, nx, ny, planes, rows, chunks),
        out_shape=(
            jax.ShapeDtypeStruct((planes, rows, cols), f32),
            jax.ShapeDtypeStruct((24, cols), f32),
        ),
        in_specs=[any_spec] * 3,
        out_specs=(any_spec, pl.BlockSpec(memory_space=pltpu.VMEM)),
        scratch_shapes=[
            padded, padded, padded, padded, plain, plain,
            pltpu.VMEM((planes + 1, chunks, rows, LANES), f32),
            pltpu.VMEM((planes, chunks, rows + 8, LANES), f32),
            plain,
            pltpu.VMEM((2 * half * chunks, 8, LANES), f32),
            pltpu.VMEM((ny, 8, LANES), f32),
            pltpu.VMEM((nx, 2, ny * half, LANES), f32),
            pltpu.VMEM((nx, ny * half, LANES), f32),
            pltpu.SemaphoreType.DMA((3,)),
            pltpu.SemaphoreType.DMA,
            pltpu.SemaphoreType.DMA((32,)),
            pltpu.SemaphoreType.DMA((32,)),
            pltpu.SemaphoreType.DMA((ny,)),
            pltpu.SemaphoreType.DMA((ny,)),
            pltpu.SemaphoreType.DMA((nx,)),
            pltpu.SemaphoreType.DMA((nx,)),
        ],
        compiler_params=pltpu.CompilerParams(
            collective_id=0, has_side_effects=True, vmem_limit_bytes=58 * 1024 * 1024
        ),
        name="correction_main",
    )(previous, source, conductivity)
    step_planes = 4
    return pl.pallas_call(
        functools.partial(add_kernel, step_planes, rows),
        out_shape=jax.ShapeDtypeStruct((planes, rows, cols), f32),
        grid=(planes // step_planes,),
        in_specs=[
            pl.BlockSpec((step_planes, rows, cols), lambda i: (i, 0, 0)),
            pl.BlockSpec((24, cols), lambda i: (0, 0)),
        ],
        out_specs=pl.BlockSpec((step_planes, rows, cols), lambda i: (i, 0, 0)),
        scratch_shapes=[pltpu.VMEM((3, rows, cols), f32)],
        compiler_params=pltpu.CompilerParams(vmem_limit_bytes=60 * 1024 * 1024),
        name="interpolate_add",
    )(fine, along)


def solution(mesh):
    placed = P("gx", "gy", None)
    nx, ny = mesh.shape["gx"], mesh.shape["gy"]
    return jax.shard_map(
        functools.partial(per_device, nx, ny), mesh=mesh, in_specs=(placed,) * 3, out_specs=placed,
        check_vma=False,
    )
```

```python
import functools

import jax
import jax.numpy as jnp
from jax import lax
from jax.experimental import pallas as pl
from jax.experimental.pallas import tpu as pltpu
from jax.sharding import PartitionSpec as P

F = 16
CSWEEPS = 32
LANES = 128
TOP = 8

reaction = 0.2
damping = 0.8
coarse_factor = 0.25

MESH = pl.DeviceIdType.MESH
HI = lax.Precision.HIGHEST


def lane_index(shape):
    return lax.broadcasted_iota(jnp.int32, shape, len(shape) - 1)


def next_col(here, after):
    first = lane_index(here.shape) == 0
    return pltpu.roll(jnp.where(first, after, here), LANES - 1, 1)


def prev_col(before, here):
    last = lane_index(here.shape) == LANES - 1
    return pltpu.roll(jnp.where(last, before, here), 1, 1)


def main_kernel(
    nx, ny, planes, rows, chunks,
    prev_hbm, src_hbm, cond_hbm, out_hbm,
    cond, prev, corr1, corr2, src, wgt, cx, cy, cz,
    acc, part, gather, coarse, across,
    load_sem, out_sem, send_sem, recv_sem, psend_sem, precv_sem, gsend_sem, grecv_sem,
):
    gx, gy = lax.axis_index("gx"), lax.axis_index("gy")
    body_rows = pl.ds(TOP, rows)
    last_row = TOP + rows - 1
    inner = planes - 2
    steps = 2 * planes

    def place_of(i):
        late = lax.div(i, 2 * inner)
        past = i - 2 * inner
        edge = (1 - late) * lax.div(i, inner) + late * lax.rem(past, 2)
        order = (1 - late) * lax.rem(i, inner) + late * (inner + lax.div(past, 2))
        return lax.rem(order + 1, planes) + 1, order, edge

    def tiles(edge):
        low = TOP + rows // 2 - 8 - (rows // 2 - 8) * edge
        high = TOP + rows // 2 + (rows // 2 - 8) * edge
        return pl.multiple_of(low, 8), pl.multiple_of(high, 8)

    def get(ref, p, c, at, shift=0):
        return jnp.concatenate([ref[p, c, pl.ds(t + shift, 8), :] for t in at], axis=0)

    def put(ref, p, c, at, block):
        ref[p, c, pl.ds(at[0], 8), :] = block[0:8]
        ref[p, c, pl.ds(at[1], 8), :] = block[8:16]

    loads = ((cond_hbm, cond, True), (prev_hbm, prev, True), (src_hbm, src, False))
    for k, (hbm, buf, padded) in enumerate(loads):
        for c in range(chunks):
            part_hbm = hbm.at[:, :, pl.ds(c * LANES, LANES)]
            dst = buf.at[pl.ds(1, planes), c, body_rows, :] if padded else buf.at[:, c]
            pltpu.make_async_copy(part_hbm, dst, load_sem.at[k]).start()

    def wait_load(k):
        pltpu.make_async_copy(src, src, load_sem.at[k]).wait()

    barrier = pltpu.get_barrier_semaphore()
    for j in range(1, nx):
        pl.semaphore_signal(barrier, inc=1, device_id=(lax.rem(gx + j, nx), gy), device_id_type=MESH)
    for j in range(1, ny):
        pl.semaphore_signal(barrier, inc=1, device_id=(gx, lax.rem(gy + j, ny)), device_id_type=MESH)
    pl.semaphore_wait(barrier, nx + ny - 2)

    x_next, x_prev = (lax.rem(gx + 1, nx), gy), (lax.rem(gx + nx - 1, nx), gy)
    y_next, y_prev = (gx, lax.rem(gy + 1, ny)), (gx, lax.rem(gy + ny - 1, ny))
    fields = (cond, prev, corr1, corr2)

    def remote(source, target, sem, device):
        return pltpu.make_async_remote_copy(
            src_ref=source, dst_ref=target, send_sem=send_sem.at[sem], recv_sem=recv_sem.at[sem],
            device_id=device, device_id_type=MESH,
        )

    def plane_copies(k):
        buf = fields[k]
        return (
            remote(buf.at[1, :, body_rows, :], buf.at[planes + 1, :, body_rows, :], 2 * k, x_prev),
            remote(buf.at[planes, :, body_rows, :], buf.at[0, :, body_rows, :], 2 * k + 1, x_next),
        )

    def row_copies(k, late):
        buf, copies = fields[k], []
        groups = ((1, 1), (planes, 1)) if late else ((2, inner),)
        for g, (first, count) in enumerate(groups):
            sem = 8 + 6 * k + (2 + 2 * g if late else 0)
            span = pl.ds(first, count)

            def row(at):
                return buf.at[span, :, pl.ds(at, 1), :]

            copies.append(remote(row(TOP), row(last_row + 1), sem, y_prev))
            copies.append(remote(row(last_row), row(TOP - 1), sem + 1, y_next))
        return tuple(copies)

    def start_all(copies):
        for copy in copies:
            copy.start()

    def wait_recv(copies):
        for copy in copies:
            copy.wait_recv()

    def arrivals(i, ks, sent=None):
        @pl.when(i == inner)
        def _():
            for k in ks:
                wait_recv(row_copies(k, 0))

        @pl.when(i == 2 * inner)
        def _():
            if sent is not None:
                start_all(row_copies(sent, 0))
            for k in ks:
                wait_recv(row_copies(k, 1))
                wait_recv(plane_copies(k))

    for k in (0, 1):
        wait_load(k)
        start_all(plane_copies(k))
        start_all(row_copies(k, 0))
        start_all(row_copies(k, 1))
    acc[...] = jnp.zeros_like(acc)

    half = rows // F

    def add_part(field, c, block):
        for r in range(half):
            at = (field * half + r) * chunks + c
            acc[at] = acc[at] + block[8 * r : 8 * r + 8]

    @pl.loop(0, steps)
    def _(i):
        p, order, edge = place_of(i)
        at = tiles(edge)
        flat = tuple(pl.multiple_of(t - TOP, 8) for t in at)
        arrivals(i, (0,))

        def cond_at(c):
            return get(cond, p, c % chunks, at)

        ready = []
        k_here = cond_at(chunks - 1)
        k_after = cond_at(0)
        cz_before = k_here + next_col(k_here, k_after)
        k_here = k_after
        for c in range(chunks):
            k_after = cond_at(c + 1)
            cz_here = k_here + next_col(k_here, k_after)
            cz_low = prev_col(cz_before, cz_here)
            cx_high = k_here + get(cond, p + 1, c, at)
            cx_low = k_here + get(cond, p - 1, c, at)
            cy_high = k_here + get(cond, p, c, at, 1)
            cy_low = k_here + get(cond, p, c, at, -1)
            twice_diag = (((cx_high + cx_low) + (cy_high + cy_low)) + (cz_here + cz_low)) + 2 * reaction
            ready.append((c, cz_here, cx_high, cx_low, cy_high, cy_low[0:1], twice_diag, k_here))
            k_here, cz_before = k_after, cz_here
            if len(ready) == 4:
                for d, c_z, c_xh, c_xl, c_yh, c_yl, twice, kept in ready:
                    put(cz, p - 1, d, flat, c_z)
                    put(cx, p, d, flat, c_xh)
                    put(cx, p - 1, d, flat, c_xl)
                    put(cy, p - 1, d, at, c_yh)
                    cy[p - 1, d, pl.ds(at[0] - 1, 1), :] = c_yl
                    put(wgt, p - 1, d, flat, twice)
                    add_part(1, d, kept)
                ready = []

    def sweep(k, buf, make, write, group, sent=None):
        @pl.loop(0, steps)
        def _(i):
            p, order, edge = place_of(i)
            at = tiles(edge)
            flat = tuple(pl.multiple_of(t - TOP, 8) for t in at)
            if k == 2:
                pl.when(i == inner // 2)(pass_on)
            arrivals(i, (k,), sent)

            def here_at(c):
                return get(buf, p, c % chunks, at)

            ready = []
            q_before = get(cz, p - 1, chunks - 1, flat) * here_at(chunks - 1)
            here = here_at(0)
            for c in range(chunks):
                after = here_at(c + 1)
                cz_here = get(cz, p - 1, c, flat)
                q_here = cz_here * here
                total = (
                    (get(cx, p, c, flat) * get(buf, p + 1, c, at) + get(cx, p - 1, c, flat) * get(buf, p - 1, c, at))
                    + (
                        get(cy, p - 1, c, at) * get(buf, p, c, at, 1)
                        + get(cy, p - 1, c, at, -1) * get(buf, p, c, at, -1)
                    )
                ) + (cz_here * next_col(here, after) + prev_col(q_before, q_here))
                ready.append((c, make(p, c, at, flat, here, total)))
                here, q_before = after, q_here
                if len(ready) == group:
                    for d, made in ready:
                        write(p, order, d, at, flat, *made)
                    ready = []

            if k == 3:
                @pl.when((i >= inner) & (i < 2 * inner) & (lax.rem(i - inner, 4) == 3))
                def _():
                    store_planes(i - inner - 2, 4)

    def make_first(p, c, at, flat, here, total):
        twice_diag = get(wgt, p - 1, c, flat)
        resid = get(src, p - 1, c, flat) - 0.5 * (twice_diag * here - total)
        weight = damping / twice_diag
        return weight, (2.0 * weight) * resid, resid

    def write_first(p, order, c, at, flat, weight, first, resid):
        put(wgt, p - 1, c, flat, weight)
        put(corr1, p, c, at, first)
        add_part(0, c, resid)

    wait_load(2)
    sweep(1, prev, make_first, write_first, 4, 2)
    start_all(plane_copies(2))
    start_all(row_copies(2, 1))

    lines = 2 * half * chunks
    sums = jnp.sum(acc[...], axis=1)
    per_chunk = LANES // F
    lane_row = lax.broadcasted_iota(jnp.int32, (LANES, LANES), 0)
    lane_col = lax.broadcasted_iota(jnp.int32, (LANES, LANES), 1)
    pool = jnp.where(lax.rem(lane_col, per_chunk) == lax.div(lane_row, F), 1.0, 0.0)
    pooled = jnp.dot(sums, pool, precision=HI, preferred_element_type=jnp.float32)
    line_row = lax.broadcasted_iota(jnp.int32, (lines, LANES), 0)
    line_col = lax.broadcasted_iota(jnp.int32, (lines, LANES), 1)
    pooled = jnp.where(lax.div(line_col, per_chunk) == lax.rem(line_row, chunks), pooled, 0.0)
    small = jnp.sum(pooled.reshape(2 * half, chunks, LANES), axis=1) * (1.0 / (F * F * F))
    part[gy, 0 : 2 * half, :] = small

    def part_copy(j):
        return pltpu.make_async_remote_copy(
            src_ref=part.at[gy], dst_ref=part.at[gy], send_sem=psend_sem.at[j], recv_sem=precv_sem.at[j],
            device_id=(gx, lax.rem(gy + j, ny)), device_id_type=MESH,
        )

    def part_arrival(j):
        at = lax.rem(gy + ny - j, ny)
        return pltpu.make_async_remote_copy(
            src_ref=part.at[at], dst_ref=part.at[at], send_sem=psend_sem.at[j], recv_sem=precv_sem.at[j],
            device_id=(gx, lax.rem(gy + j, ny)), device_id_type=MESH,
        )

    def gather_copy(j):
        return pltpu.make_async_remote_copy(
            src_ref=gather.at[gx], dst_ref=gather.at[gx], send_sem=gsend_sem.at[j], recv_sem=grecv_sem.at[j],
            device_id=(lax.rem(gx + j, nx), gy), device_id_type=MESH,
        )

    def gather_arrival(j):
        at = lax.rem(gx + nx - j, nx)
        return pltpu.make_async_remote_copy(
            src_ref=gather.at[at], dst_ref=gather.at[at], send_sem=gsend_sem.at[j], recv_sem=grecv_sem.at[j],
            device_id=(lax.rem(gx + j, nx), gy), device_id_type=MESH,
        )

    for j in range(1, ny):
        part_copy(j).start()

    def pass_on():
        for j in range(1, ny):
            part_arrival(j).wait_recv()
        for y in range(ny):
            for f in range(2):
                gather[gx, f, y * half : (y + 1) * half, :] = part[y, f * half : (f + 1) * half, :]
        for j in range(1, nx):
            gather_copy(j).start()

    def make_second(p, c, at, flat, here, total):
        return ((1.0 + (1.0 - damping)) * here + get(wgt, p - 1, c, flat) * total,)

    def write_second(p, order, c, at, flat, second):
        put(corr2, p, c, at, second)

    sweep(2, corr1, make_second, write_second, 8, 3)
    start_all(plane_copies(3))
    start_all(row_copies(3, 1))

    for j in range(1, nx):
        gather_arrival(j).wait_recv()
    crows = ny * half
    resid = gather[:, 0]
    ccond = gather[:, 1]

    def around(v):
        return (
            jnp.concatenate([v[1:], v[:1]], axis=0), jnp.concatenate([v[-1:], v[:-1]], axis=0),
            pltpu.roll(v, crows - 1, 1), pltpu.roll(v, 1, 1),
            pltpu.roll(v, 1, 2), pltpu.roll(v, LANES - 1, 2),
        )

    ccoup = [(0.5 * coarse_factor) * (ccond + near) for near in around(ccond)]
    cdiag = jnp.full_like(ccond, reaction)
    for one in ccoup:
        cdiag = cdiag + one
    cwgt = damping / cdiag
    ccoup = [cwgt * one for one in ccoup]
    cfirst = cwgt * resid

    def coarse_step(_, v):
        result = (1.0 - damping) * v + cfirst
        for one, near in zip(ccoup, around(v)):
            result = result + one * near
        return result

    coarse[...] = lax.fori_loop(0, CSWEEPS - 1, coarse_step, cfirst)
    turn = lax.rem(2 * crows + 1 - gy * half, crows)
    block = []
    for a in range(3):
        plane = coarse[lax.rem(gx + nx - 1 + a, nx)]
        block.append(pltpu.roll(plane, turn, 0)[0:8])
    block = jnp.concatenate(block, axis=0)
    ccols = chunks * LANES // F
    row = lax.broadcasted_iota(jnp.int32, (rows, LANES), 0)
    row_base = lax.div(row, F) + 1
    row_offset = (lax.rem(row, F).astype(jnp.float32) + 0.5) / F - 0.5
    row_side = jnp.where(row_offset > 0, row_base + 1, row_base - 1)
    row_weights = [
        jnp.where(row_base == b, 1.0 - jnp.abs(row_offset), 0.0)
        + jnp.where(row_side == b, jnp.abs(row_offset), 0.0)
        for b in range(half + 2)
    ]
    for c in range(chunks):
        fine = c * LANES + lane_col
        base = lax.div(fine, F)
        offset = (lax.rem(fine, F).astype(jnp.float32) + 0.5) / F - 0.5
        side = lax.rem(jnp.where(offset > 0, base + 1, base + ccols - 1), ccols)
        spread = jnp.where(lane_row == base, 1.0 - jnp.abs(offset), 0.0)
        spread = spread + jnp.where(lane_row == side, jnp.abs(offset), 0.0)
        along = jnp.dot(block, spread, precision=HI, preferred_element_type=jnp.float32)
        for a in range(3):
            total = row_weights[0] * along[8 * a : 8 * a + 1]
            for b in range(1, half + 2):
                total = total + row_weights[b] * along[8 * a + b : 8 * a + b + 1]
            across[a, c] = total

    def out_copy(c, start, count):
        return pltpu.make_async_copy(
            src.at[pl.ds(start, count), c],
            out_hbm.at[pl.ds(start, count), :, pl.ds(c * LANES, LANES)],
            out_sem,
        )

    def store_planes(start, count):
        for c in range(chunks):
            out_copy(c, start, count).start()

    def make_third(p, c, at, flat, here, total):
        term = get(wgt, p - 1, c, flat) * total
        side = 2 * lax.div(p - 1, F // 2)
        weight = jnp.abs(((p - 1).astype(jnp.float32) + 0.5) / F - 0.5)
        inter = (1.0 - weight) * get(across, 1, c, flat) + weight * get(across, side, c, flat)
        return ((((1.0 - damping) * here + get(corr1, p, c, at)) + term) + inter,)

    def write_third(p, order, c, at, flat, third):
        put(src, p - 1, c, flat, third)

    sweep(3, corr2, make_third, write_third, 8)
    store_planes(planes - 3, 3)
    store_planes(0, 1)

    for k in range(4):
        for copy in plane_copies(k) + row_copies(k, 0) + row_copies(k, 1):
            copy.wait_send()
    for j in range(1, ny):
        part_copy(j).wait_send()
    for j in range(1, nx):
        gather_copy(j).wait_send()
    pltpu.make_async_copy(src, src, out_sem).wait()


def per_device(nx, ny, previous, source, conductivity):
    planes, rows, cols = previous.shape
    chunks = cols // LANES
    half = rows // F
    f32 = jnp.float32
    padded = pltpu.VMEM((planes + 2, chunks, rows + 16, LANES), f32)
    plain = pltpu.VMEM((planes, chunks, rows, LANES), f32)
    any_spec = pl.BlockSpec(memory_space=pl.ANY)
    return pl.pallas_call(
        functools.partial(main_kernel, nx, ny, planes, rows, chunks),
        out_shape=jax.ShapeDtypeStruct((planes, rows, cols), f32),
        in_specs=[any_spec] * 3,
        out_specs=any_spec,
        scratch_shapes=[
            padded, padded, padded, padded, plain, plain,
            pltpu.VMEM((planes + 1, chunks, rows, LANES), f32),
            pltpu.VMEM((planes, chunks, rows + 8, LANES), f32),
            plain,
            pltpu.VMEM((2 * half * chunks, 8, LANES), f32),
            pltpu.VMEM((ny, 8, LANES), f32),
            pltpu.VMEM((nx, 2, ny * half, LANES), f32),
            pltpu.VMEM((nx, ny * half, LANES), f32),
            pltpu.VMEM((3, chunks, rows, LANES), f32),
            pltpu.SemaphoreType.DMA((3,)),
            pltpu.SemaphoreType.DMA,
            pltpu.SemaphoreType.DMA((32,)),
            pltpu.SemaphoreType.DMA((32,)),
            pltpu.SemaphoreType.DMA((ny,)),
            pltpu.SemaphoreType.DMA((ny,)),
            pltpu.SemaphoreType.DMA((nx,)),
            pltpu.SemaphoreType.DMA((nx,)),
        ],
        compiler_params=pltpu.CompilerParams(
            collective_id=0, has_side_effects=True, vmem_limit_bytes=58 * 1024 * 1024
        ),
        name="correction_main",
    )(previous, source, conductivity)


def solution(mesh):
    placed = P("gx", "gy", None)
    nx, ny = mesh.shape["gx"], mesh.shape["gy"]
    return jax.shard_map(
        functools.partial(per_device, nx, ny), mesh=mesh, in_specs=(placed,) * 3, out_specs=placed,
        check_vma=False,
    )
```

```python
import functools

import jax
import jax.numpy as jnp
from jax import lax
from jax.experimental import pallas as pl
from jax.experimental.pallas import tpu as pltpu
from jax.sharding import PartitionSpec as P

F = 16
CSWEEPS = 32
LANES = 128
TOP = 8

reaction = 0.2
damping = 0.8
coarse_factor = 0.25

MESH = pl.DeviceIdType.MESH
HI = lax.Precision.HIGHEST


def lane_index(shape):
    return lax.broadcasted_iota(jnp.int32, shape, len(shape) - 1)


def next_col(here, after):
    first = lane_index(here.shape) == 0
    return pltpu.roll(jnp.where(first, after, here), LANES - 1, 1)


def prev_col(before, here):
    last = lane_index(here.shape) == LANES - 1
    return pltpu.roll(jnp.where(last, before, here), 1, 1)


def main_kernel(
    nx, ny, planes, rows, chunks,
    prev_hbm, src_hbm, cond_hbm, out_hbm, cols_ref,
    cond, prev, corr1, corr2, src, wgt, cx, cy, cz,
    acc, part, gather, coarse,
    load_sem, out_sem, send_sem, recv_sem, psend_sem, precv_sem, gsend_sem, grecv_sem,
):
    gx, gy = lax.axis_index("gx"), lax.axis_index("gy")
    body_rows = pl.ds(TOP, rows)
    last_row = TOP + rows - 1
    inner = planes - 2
    steps = 2 * planes

    def place_of(i):
        late = lax.div(i, 2 * inner)
        past = i - 2 * inner
        edge = (1 - late) * lax.div(i, inner) + late * lax.rem(past, 2)
        order = (1 - late) * lax.rem(i, inner) + late * (inner + lax.div(past, 2))
        return lax.rem(order + 1, planes) + 1, order, edge

    def tiles(edge):
        low = TOP + rows // 2 - 8 - (rows // 2 - 8) * edge
        high = TOP + rows // 2 + (rows // 2 - 8) * edge
        return pl.multiple_of(low, 8), pl.multiple_of(high, 8)

    def get(ref, p, c, at, shift=0):
        return jnp.concatenate([ref[p, c, pl.ds(t + shift, 8), :] for t in at], axis=0)

    def put(ref, p, c, at, block):
        ref[p, c, pl.ds(at[0], 8), :] = block[0:8]
        ref[p, c, pl.ds(at[1], 8), :] = block[8:16]

    loads = ((cond_hbm, cond, True), (prev_hbm, prev, True), (src_hbm, src, False))
    for k, (hbm, buf, padded) in enumerate(loads):
        for c in range(chunks):
            part_hbm = hbm.at[:, :, pl.ds(c * LANES, LANES)]
            dst = buf.at[pl.ds(1, planes), c, body_rows, :] if padded else buf.at[:, c]
            pltpu.make_async_copy(part_hbm, dst, load_sem.at[k]).start()

    def wait_load(k):
        pltpu.make_async_copy(src, src, load_sem.at[k]).wait()

    barrier = pltpu.get_barrier_semaphore()
    for j in range(1, nx):
        pl.semaphore_signal(barrier, inc=1, device_id=(lax.rem(gx + j, nx), gy), device_id_type=MESH)
    for j in range(1, ny):
        pl.semaphore_signal(barrier, inc=1, device_id=(gx, lax.rem(gy + j, ny)), device_id_type=MESH)
    pl.semaphore_wait(barrier, nx + ny - 2)

    x_next, x_prev = (lax.rem(gx + 1, nx), gy), (lax.rem(gx + nx - 1, nx), gy)
    y_next, y_prev = (gx, lax.rem(gy + 1, ny)), (gx, lax.rem(gy + ny - 1, ny))
    fields = (cond, prev, corr1, corr2)

    def remote(source, target, sem, device):
        return pltpu.make_async_remote_copy(
            src_ref=source, dst_ref=target, send_sem=send_sem.at[sem], recv_sem=recv_sem.at[sem],
            device_id=device, device_id_type=MESH,
        )

    def plane_copies(k):
        buf = fields[k]
        return (
            remote(buf.at[1, :, body_rows, :], buf.at[planes + 1, :, body_rows, :], 2 * k, x_prev),
            remote(buf.at[planes, :, body_rows, :], buf.at[0, :, body_rows, :], 2 * k + 1, x_next),
        )

    def row_copies(k, late):
        buf, copies = fields[k], []
        groups = ((1, 1), (planes, 1)) if late else ((2, inner),)
        for g, (first, count) in enumerate(groups):
            sem = 8 + 6 * k + (2 + 2 * g if late else 0)
            span = pl.ds(first, count)

            def row(at):
                return buf.at[span, :, pl.ds(at, 1), :]

            copies.append(remote(row(TOP), row(last_row + 1), sem, y_prev))
            copies.append(remote(row(last_row), row(TOP - 1), sem + 1, y_next))
        return tuple(copies)

    def start_all(copies):
        for copy in copies:
            copy.start()

    def wait_recv(copies):
        for copy in copies:
            copy.wait_recv()

    def arrivals(i, ks, sent=None):
        @pl.when(i == inner)
        def _():
            for k in ks:
                wait_recv(row_copies(k, 0))

        @pl.when(i == 2 * inner)
        def _():
            if sent is not None:
                start_all(row_copies(sent, 0))
            for k in ks:
                wait_recv(row_copies(k, 1))
                wait_recv(plane_copies(k))

    for k in (0, 1):
        wait_load(k)
        start_all(plane_copies(k))
        start_all(row_copies(k, 0))
        start_all(row_copies(k, 1))
    acc[...] = jnp.zeros_like(acc)
    wait_load(2)

    half = rows // F

    def add_part(field, c, block):
        for r in range(half):
            at = (field * half + r) * chunks + c
            acc[at] = acc[at] + block[8 * r : 8 * r + 8]

    @pl.loop(0, steps)
    def _(i):
        p, order, edge = place_of(i)
        at = tiles(edge)
        flat = tuple(pl.multiple_of(t - TOP, 8) for t in at)
        arrivals(i, (0, 1), 2)

        def cond_at(c):
            return get(cond, p, c % chunks, at)

        def prev_at(c):
            return get(prev, p, c % chunks, at)

        k_here = cond_at(chunks - 1)
        k_after = cond_at(0)
        cz_before = k_here + next_col(k_here, k_after)
        q_before = cz_before * prev_at(chunks - 1)
        k_here = k_after
        v_here = prev_at(0)
        for c in range(chunks):
            k_after, v_after = cond_at(c + 1), prev_at(c + 1)
            cz_here = k_here + next_col(k_here, k_after)
            q_here = cz_here * v_here
            cz_low = prev_col(cz_before, cz_here)
            cx_high = k_here + get(cond, p + 1, c, at)
            cx_low = k_here + get(cond, p - 1, c, at)
            cy_high = k_here + get(cond, p, c, at, 1)
            cy_low = k_here + get(cond, p, c, at, -1)
            put(cz, p - 1, c, flat, cz_here)
            put(cx, p, c, flat, cx_high)
            put(cx, p - 1, c, flat, cx_low)
            put(cy, p - 1, c, at, cy_high)
            cy[p - 1, c, pl.ds(at[0] - 1, 1), :] = cy_low[0:1]
            twice_diag = (((cx_high + cx_low) + (cy_high + cy_low)) + (cz_here + cz_low)) + 2 * reaction
            total = (
                (cx_high * get(prev, p + 1, c, at) + cx_low * get(prev, p - 1, c, at))
                + (cy_high * get(prev, p, c, at, 1) + cy_low * get(prev, p, c, at, -1))
            ) + (cz_here * next_col(v_here, v_after) + prev_col(q_before, q_here))
            resid = get(src, p - 1, c, flat) - 0.5 * (twice_diag * v_here - total)
            weight = damping / twice_diag
            first = (2.0 * weight) * resid
            put(wgt, p - 1, c, flat, weight)
            put(corr1, p, c, at, first)
            add_part(0, c, resid)
            add_part(1, c, k_here)
            k_here, v_here, cz_before, q_before = k_after, v_after, cz_here, q_here

    start_all(plane_copies(2))
    start_all(row_copies(2, 1))

    lines = 2 * half * chunks
    sums = jnp.sum(acc[...], axis=1)
    per_chunk = LANES // F
    lane_row = lax.broadcasted_iota(jnp.int32, (LANES, LANES), 0)
    lane_col = lax.broadcasted_iota(jnp.int32, (LANES, LANES), 1)
    pool = jnp.where(lax.rem(lane_col, per_chunk) == lax.div(lane_row, F), 1.0, 0.0)
    pooled = jnp.dot(sums, pool, precision=HI, preferred_element_type=jnp.float32)
    line_row = lax.broadcasted_iota(jnp.int32, (lines, LANES), 0)
    line_col = lax.broadcasted_iota(jnp.int32, (lines, LANES), 1)
    pooled = jnp.where(lax.div(line_col, per_chunk) == lax.rem(line_row, chunks), pooled, 0.0)
    small = jnp.sum(pooled.reshape(2 * half, chunks, LANES), axis=1) * (1.0 / (F * F * F))
    part[gy, 0 : 2 * half, :] = small

    def part_copy(j):
        return pltpu.make_async_remote_copy(
            src_ref=part.at[gy], dst_ref=part.at[gy], send_sem=psend_sem.at[j], recv_sem=precv_sem.at[j],
            device_id=(gx, lax.rem(gy + j, ny)), device_id_type=MESH,
        )

    def part_arrival(j):
        at = lax.rem(gy + ny - j, ny)
        return pltpu.make_async_remote_copy(
            src_ref=part.at[at], dst_ref=part.at[at], send_sem=psend_sem.at[j], recv_sem=precv_sem.at[j],
            device_id=(gx, lax.rem(gy + j, ny)), device_id_type=MESH,
        )

    def gather_copy(j):
        return pltpu.make_async_remote_copy(
            src_ref=gather.at[gx], dst_ref=gather.at[gx], send_sem=gsend_sem.at[j], recv_sem=grecv_sem.at[j],
            device_id=(lax.rem(gx + j, nx), gy), device_id_type=MESH,
        )

    def gather_arrival(j):
        at = lax.rem(gx + nx - j, nx)
        return pltpu.make_async_remote_copy(
            src_ref=gather.at[at], dst_ref=gather.at[at], send_sem=gsend_sem.at[j], recv_sem=grecv_sem.at[j],
            device_id=(lax.rem(gx + j, nx), gy), device_id_type=MESH,
        )

    for j in range(1, ny):
        part_copy(j).start()

    def pass_on():
        for j in range(1, ny):
            part_arrival(j).wait_recv()
        for y in range(ny):
            for f in range(2):
                gather[gx, f, y * half : (y + 1) * half, :] = part[y, f * half : (f + 1) * half, :]
        for j in range(1, nx):
            gather_copy(j).start()

    def sweep(k, buf, write, sent=None):
        @pl.loop(0, steps)
        def _(i):
            p, order, edge = place_of(i)
            at = tiles(edge)
            flat = tuple(pl.multiple_of(t - TOP, 8) for t in at)
            if k == 2:
                pl.when(i == inner // 2)(pass_on)
            arrivals(i, (k,), sent)

            def here_at(c):
                return get(buf, p, c % chunks, at)

            q_before = get(cz, p - 1, chunks - 1, flat) * here_at(chunks - 1)
            here = here_at(0)
            for c in range(chunks):
                after = here_at(c + 1)
                cz_here = get(cz, p - 1, c, flat)
                q_here = cz_here * here
                total = (
                    (get(cx, p, c, flat) * get(buf, p + 1, c, at) + get(cx, p - 1, c, flat) * get(buf, p - 1, c, at))
                    + (
                        get(cy, p - 1, c, at) * get(buf, p, c, at, 1)
                        + get(cy, p - 1, c, at, -1) * get(buf, p, c, at, -1)
                    )
                ) + (cz_here * next_col(here, after) + prev_col(q_before, q_here))
                write(p, order, c, at, flat, here, get(wgt, p - 1, c, flat) * total)
                here, q_before = after, q_here

            if k == 3:
                @pl.when((i >= inner) & (i < 2 * inner) & (lax.rem(i - inner, 4) == 3))
                def _():
                    store_planes(i - inner - 2, 4)

    def write_second(p, order, c, at, flat, here, term):
        second = (1.0 + (1.0 - damping)) * here + term
        put(corr2, p, c, at, second)

    sweep(2, corr1, write_second, 3)
    start_all(plane_copies(3))
    start_all(row_copies(3, 1))

    for j in range(1, nx):
        gather_arrival(j).wait_recv()
    crows = ny * half
    resid = gather[:, 0]
    ccond = gather[:, 1]

    def around(v):
        return (
            jnp.concatenate([v[1:], v[:1]], axis=0), jnp.concatenate([v[-1:], v[:-1]], axis=0),
            pltpu.roll(v, crows - 1, 1), pltpu.roll(v, 1, 1),
            pltpu.roll(v, 1, 2), pltpu.roll(v, LANES - 1, 2),
        )

    ccoup = [(0.5 * coarse_factor) * (ccond + near) for near in around(ccond)]
    cdiag = jnp.full_like(ccond, reaction)
    for one in ccoup:
        cdiag = cdiag + one
    cwgt = damping / cdiag
    ccoup = [cwgt * one for one in ccoup]
    cfirst = cwgt * resid

    def coarse_step(_, v):
        result = (1.0 - damping) * v + cfirst
        for one, near in zip(ccoup, around(v)):
            result = result + one * near
        return result

    coarse[...] = lax.fori_loop(0, CSWEEPS - 1, coarse_step, cfirst)
    turn = lax.rem(2 * crows + 1 - gy * half, crows)
    block = []
    for a in range(3):
        plane = coarse[lax.rem(gx + nx - 1 + a, nx)]
        block.append(pltpu.roll(plane, turn, 0)[0:8])
    block = jnp.concatenate(block, axis=0)
    ccols = chunks * LANES // F
    for c in range(chunks):
        fine = c * LANES + lane_col
        base = lax.div(fine, F)
        offset = (lax.rem(fine, F).astype(jnp.float32) + 0.5) / F - 0.5
        side = lax.rem(jnp.where(offset > 0, base + 1, base + ccols - 1), ccols)
        spread = jnp.where(lane_row == base, 1.0 - jnp.abs(offset), 0.0)
        spread = spread + jnp.where(lane_row == side, jnp.abs(offset), 0.0)
        cols_ref[:, c * LANES : (c + 1) * LANES] = jnp.dot(
            block, spread, precision=HI, preferred_element_type=jnp.float32
        )

    def out_copy(c, start, count):
        return pltpu.make_async_copy(
            src.at[pl.ds(start, count), c],
            out_hbm.at[pl.ds(start, count), :, pl.ds(c * LANES, LANES)],
            out_sem,
        )

    def store_planes(start, count):
        for c in range(chunks):
            out_copy(c, start, count).start()

    def write_third(p, order, c, at, flat, here, term):
        put(src, p - 1, c, flat, ((1.0 - damping) * here + get(corr1, p, c, at)) + term)

    sweep(3, corr2, write_third)
    store_planes(planes - 3, 3)
    store_planes(0, 1)

    for k in range(4):
        for copy in plane_copies(k) + row_copies(k, 0) + row_copies(k, 1):
            copy.wait_send()
    for j in range(1, ny):
        part_copy(j).wait_send()
    for j in range(1, nx):
        gather_copy(j).wait_send()
    pltpu.make_async_copy(src, src, out_sem).wait()


def add_kernel(step_planes, rows, fine_ref, cols_ref, out_ref, across):
    step = pl.program_id(0)
    half = rows // F

    @pl.when(step == 0)
    def _():
        row = lax.broadcasted_iota(jnp.int32, (rows, LANES), 0)
        base = lax.div(row, F) + 1
        offset = (lax.rem(row, F).astype(jnp.float32) + 0.5) / F - 0.5
        side = jnp.where(offset > 0, base + 1, base - 1)
        weights = [
            jnp.where(base == b, 1.0 - jnp.abs(offset), 0.0) + jnp.where(side == b, jnp.abs(offset), 0.0)
            for b in range(half + 2)
        ]
        for a in range(3):
            for c in range(cols_ref.shape[1] // LANES):
                at = pl.ds(c * LANES, LANES)
                total = weights[0] * cols_ref[8 * a : 8 * a + 1, at]
                for b in range(1, half + 2):
                    total = total + weights[b] * cols_ref[8 * a + b : 8 * a + b + 1, at]
                across[a, :, at] = total

    for q in range(step_planes):
        plane = step * step_planes + q
        offset = (plane.astype(jnp.float32) + 0.5) / F - 0.5
        side = jnp.where(offset > 0, 2, 0)
        weight = jnp.abs(offset)
        out_ref[q] = fine_ref[q] + ((1.0 - weight) * across[1] + weight * across[side])


def per_device(nx, ny, previous, source, conductivity):
    planes, rows, cols = previous.shape
    chunks = cols // LANES
    half = rows // F
    f32 = jnp.float32
    padded = pltpu.VMEM((planes + 2, chunks, rows + 16, LANES), f32)
    plain = pltpu.VMEM((planes, chunks, rows, LANES), f32)
    any_spec = pl.BlockSpec(memory_space=pl.ANY)
    fine, along = pl.pallas_call(
        functools.partial(main_kernel, nx, ny, planes, rows, chunks),
        out_shape=(
            jax.ShapeDtypeStruct((planes, rows, cols), f32),
            jax.ShapeDtypeStruct((24, cols), f32),
        ),
        in_specs=[any_spec] * 3,
        out_specs=(any_spec, pl.BlockSpec(memory_space=pltpu.VMEM)),
        scratch_shapes=[
            padded, padded, padded, padded, plain, plain,
            pltpu.VMEM((planes + 1, chunks, rows, LANES), f32),
            pltpu.VMEM((planes, chunks, rows + 8, LANES), f32),
            plain,
            pltpu.VMEM((2 * half * chunks, 8, LANES), f32),
            pltpu.VMEM((ny, 8, LANES), f32),
            pltpu.VMEM((nx, 2, ny * half, LANES), f32),
            pltpu.VMEM((nx, ny * half, LANES), f32),
            pltpu.SemaphoreType.DMA((3,)),
            pltpu.SemaphoreType.DMA,
            pltpu.SemaphoreType.DMA((32,)),
            pltpu.SemaphoreType.DMA((32,)),
            pltpu.SemaphoreType.DMA((ny,)),
            pltpu.SemaphoreType.DMA((ny,)),
            pltpu.SemaphoreType.DMA((nx,)),
            pltpu.SemaphoreType.DMA((nx,)),
        ],
        compiler_params=pltpu.CompilerParams(
            collective_id=0, has_side_effects=True, vmem_limit_bytes=60 * 1024 * 1024
        ),
        name="correction_main",
    )(previous, source, conductivity)
    step_planes = 4
    return pl.pallas_call(
        functools.partial(add_kernel, step_planes, rows),
        out_shape=jax.ShapeDtypeStruct((planes, rows, cols), f32),
        grid=(planes // step_planes,),
        in_specs=[
            pl.BlockSpec((step_planes, rows, cols), lambda i: (i, 0, 0)),
            pl.BlockSpec((24, cols), lambda i: (0, 0)),
        ],
        out_specs=pl.BlockSpec((step_planes, rows, cols), lambda i: (i, 0, 0)),
        scratch_shapes=[pltpu.VMEM((3, rows, cols), f32)],
        compiler_params=pltpu.CompilerParams(vmem_limit_bytes=60 * 1024 * 1024),
        name="interpolate_add",
    )(fine, along)


def solution(mesh):
    placed = P("gx", "gy", None)
    nx, ny = mesh.shape["gx"], mesh.shape["gy"]
    return jax.shard_map(
        functools.partial(per_device, nx, ny), mesh=mesh, in_specs=(placed,) * 3, out_specs=placed,
        check_vma=False,
    )
```
